32 devices in a mesh: mod: 32 (over z, y, x, core).
Axes of the slice: x: 2, y: 2, z: 4, core: 2. Of those that a mesh axis runs over, the one named last changes fastest.
Arguments:
- loads: bfloat16 [32, 32768], P(None, 'mod')
- modes: float32 [6, 32768], P(None, 'mod'), may hold values from -0.6 to 0.6
- pinv: bfloat16 [32768, 1024], P('mod')
- schur: bfloat16 [32768, 1024], P('mod')
- coarse_inverse: float32 [192, 192], P('mod')
- connectors: int32 [32, 3, 8], P('mod'), may hold values from -1 to 4, as said below
Outputs:
- multipliers: float32 [32, 32768], P(None, 'mod')
The draws below stay inside these ranges and needn't reach their ends.
Inputs may be any that keep to these rules, and one draw needn't show every extreme that they name: connectors[s, 0, b] is 0 for an unused block, or 1, 2, 3, 4 when the block is tied to module s + 1, s - 1, s + 8, s - 8; its partner is the block of that module with the opposite direction (1 with 2, 3 with 4) and the same slot connectors[s, 1, b], which is below 2 (0 on unused blocks). connectors[s, 2, b] is +1 or -1 on used blocks, opposite at the two ends of a connector, and 0 on unused ones. Partners stay within rows of 8 modules along the first kind of direction and within the modules along the second. A module uses at most 2 blocks towards one neighbour, and some module uses 2.
All inputs are finite; a program needn't handle non-finite values.
Results may differ from the reference program's by a relative error of at most 0.0015.
Values sent between devices are 32-bit elements; how exact they have to be, the bound alone decides.
No kernel may reach another device: no remote copies, remote signals or barrier semaphores. Data moves between devices by JAX's collectives and lax.ppermute only.
A program may use at most 64 MiB of HBM per device.

```python
import math
import jax
import jax.numpy as jnp
from jax import lax

BLOCK = 128
BLOCKS = 8
NB = 1024
MODES = 6
MAXC = 2
ACROSS = 8
CASES = 32
ITERS = 1
MODULES = 32
COARSE = 192


def definite_blocks(key):

    def single(one_key):
        jitter_key, scale_key = jax.random.split(one_key)
        jitter = jax.random.normal(jitter_key, (NB, NB), jnp.float32) * (0.25 / math.sqrt(NB))
        scales = jnp.exp(jax.random.uniform(scale_key, (NB,), jnp.float32, 0.0, math.log(2.0)))
        matrix = jnp.eye(NB, dtype=jnp.float32) + jitter + jitter.T
        return scales[:, None] * matrix * scales[None, :]
    stacked = lax.map(single, jax.random.split(key, MODULES))
    return stacked.reshape(MODULES * NB, NB).astype(jnp.bfloat16)


def draw_pinv(key, part):
    return definite_blocks(jax.random.fold_in(key, 11))


def draw_schur(key, part):
    return definite_blocks(jax.random.fold_in(key, 12))


def draw_loads(key, part):
    key_base, key_rows, key_cols = jax.random.split(jax.random.fold_in(key, 21), 3)
    dof_total = MODULES * NB
    baseline = jax.random.normal(key_base, (CASES, dof_total), jnp.float32)
    row_scale = jnp.exp(jax.random.uniform(key_rows, (1, dof_total), jnp.float32, math.log(0.5), math.log(2.0)))
    col_scale = jnp.exp(jax.random.uniform(key_cols, (CASES, 1), jnp.float32, math.log(0.5), math.log(2.0)))
    module_ids = (jnp.arange(dof_total, dtype=jnp.int32) // NB).astype(jnp.float32)
    ramp = 0.5 * (1.0 + 2.0 * module_ids / max(MODULES - 1, 1))
    return (baseline * row_scale * col_scale * ramp[None, :]).astype(jnp.bfloat16)


def draw_coarse_inverse(key, part):
    jitter = jax.random.normal(jax.random.fold_in(key, 31), (COARSE, COARSE), jnp.float32) / math.sqrt(COARSE)
    return 0.6 * (jnp.eye(COARSE, dtype=jnp.float32) + 0.5 * (jitter + jitter.T))


def draw_connectors(key, part):
    keys = jax.random.split(jax.random.fold_in(key, 41), 5)
    module_ids = jnp.arange(MODULES, dtype=jnp.int32)
    scores = jax.random.randint(keys[0], (MODULES, BLOCKS), 0, 1 << 20) * BLOCKS + jnp.arange(BLOCKS, dtype=jnp.int32)[None, :]
    position = jnp.argsort(jnp.argsort(scores, axis=1), axis=1).astype(jnp.int32)
    link_next = jax.random.randint(keys[1], (MODULES,), 0, MAXC + 1)
    link_next = jnp.where(module_ids % ACROSS == ACROSS - 1, 0, link_next).at[0].set(MAXC)
    link_far = jax.random.randint(keys[2], (MODULES,), 0, MAXC + 1)
    link_far = jnp.where(module_ids >= MODULES - ACROSS, 0, link_far).at[0].set(MAXC)
    sign_next = 2 * jax.random.randint(keys[3], (MODULES,), 0, 2) - 1
    sign_far = 2 * jax.random.randint(keys[4], (MODULES,), 0, 2) - 1
    zero_one = jnp.zeros((1,), jnp.int32)
    zero_row = jnp.zeros((ACROSS,), jnp.int32)
    counts = jnp.stack([link_next, jnp.concatenate([zero_one, link_next[:-1]]), link_far, jnp.concatenate([zero_row, link_far[:-ACROSS]])], axis=1)
    orients = jnp.stack([sign_next, -jnp.concatenate([zero_one + 1, sign_next[:-1]]), sign_far, -jnp.concatenate([zero_row + 1, sign_far[:-ACROSS]])], axis=1)
    heading = position // MAXC
    slot_ids = position % MAXC
    live = slot_ids < jnp.take_along_axis(counts, heading, axis=1)
    heading_code = jnp.where(live, heading + 1, 0)
    slot_code = jnp.where(live, slot_ids, 0)
    orient_code = jnp.where(live, jnp.take_along_axis(orients, heading, axis=1), 0)
    return jnp.stack([heading_code, slot_code, orient_code], axis=1).astype(jnp.int32)


def level_of(own_key, shape, pieces, least, high):
    factor_of = 1.0
    for axis_at, blocks in pieces:
        steps = jax.random.uniform(jax.random.fold_in(jax.random.fold_in(own_key, 6), axis_at), (blocks,), jnp.float32, least / len(pieces), high / len(pieces))
        factor_of = factor_of * jnp.repeat(jnp.exp(steps), shape[axis_at] // blocks).reshape((-1,) + (1,) * (len(shape) - 1 - axis_at))
    return factor_of


def normal_values(key, shape, width, bound, shards=(), kind=jnp.bfloat16):
    drawn = width * jax.random.normal(key, shape, jnp.float32)
    if shards:
        drawn = drawn * level_of(key, shape, shards, -0.22, 0.18)
    return jnp.clip(drawn, -bound, bound).astype(kind)


def setup_inputs(seed: int = 0) -> dict:
    arg_keys = jax.random.split(jax.random.key(seed), 7)
    loads = draw_loads(jax.random.fold_in(arg_keys[6], 71), 0)
    modes = normal_values(arg_keys[1], (MODES, MODULES * NB), 0.1, 0.6, ((1, 32),), jnp.float32)
    pinv = draw_pinv(jax.random.fold_in(arg_keys[6], 71), 0)
    schur = draw_schur(jax.random.fold_in(arg_keys[6], 71), 0)
    coarse_inverse = draw_coarse_inverse(jax.random.fold_in(arg_keys[6], 71), 0)
    connectors = draw_connectors(jax.random.fold_in(arg_keys[6], 71), 0)
    return dict(loads=loads, modes=modes, pinv=pinv, schur=schur, coarse_inverse=coarse_inverse, connectors=connectors)


highest = lax.Precision.HIGHEST


def selector_table(connectors):
    headings = connectors[:, 0, :]
    slot_ids = connectors[:, 1, :]
    heading_ids = jnp.arange(4, dtype=jnp.int32)[:, None, None, None] + 1
    slot_range = jnp.arange(MAXC, dtype=jnp.int32)[None, :, None, None]
    return ((headings[None, None] == heading_ids) & (slot_ids[None, None] == slot_range)).astype(jnp.float32)


def shift_modules(values_in, offset):
    module_total = values_in.shape[2]
    if offset > 0:
        padding = jnp.zeros_like(values_in[:, :, :offset])
        return jnp.concatenate([padding, values_in[:, :, :module_total - offset]], axis=2)
    padding = jnp.zeros_like(values_in[:, :, :(-offset)])
    return jnp.concatenate([values_in[:, :, -offset:], padding], axis=2)


def jump_blocks(values_in, orient, selector):
    signed = values_in * orient[None, :, :, None]
    offsets = [1, -1, ACROSS, -ACROSS]
    summed = signed
    for heading in range(4):
        packed = jnp.einsum("knb,cnbe->kcne", selector[heading ^ 1], signed, precision=highest)
        received = shift_modules(packed, -offsets[heading])
        summed = summed + jnp.einsum("knb,kcne->cnbe", selector[heading], received, precision=highest)
    return summed


def reference(loads, modes, pinv, schur, coarse_inverse, connectors):
    case_count = loads.shape[0]
    block_view = (case_count, MODULES, BLOCKS, BLOCK)
    flat_view = (case_count, MODULES, NB)
    orient = connectors[:, 2, :].astype(jnp.float32)
    orient_flat = jnp.repeat(orient, BLOCK, axis=1)[None]
    selector = selector_table(connectors)
    mode_view = modes.reshape(MODES, MODULES, NB)
    pinv_view = pinv.reshape(MODULES, NB, NB)
    schur_view = schur.reshape(MODULES, NB, NB)

    def apply_jump(values_in):
        return jump_blocks(values_in.reshape(block_view), orient, selector).reshape(flat_view)

    def coarse_rhs(values_in):
        return jnp.einsum("ine,cne->nic", mode_view, values_in, precision=highest).reshape(COARSE, case_count)

    def lift(right_side):
        amplitude = jnp.dot(coarse_inverse, right_side, precision=highest).reshape(MODULES, MODES, case_count)
        return jnp.einsum("nic,ine->cne", amplitude, mode_view, precision=highest)

    def project(values_in):
        return values_in - apply_jump(lift(coarse_rhs(orient_flat * values_in)))

    def module_product(left, matrices):
        def single(pair):
            return jnp.dot(pair[0], pair[1], preferred_element_type=jnp.float32)
        result = lax.map(single, (jnp.swapaxes(left, 0, 1), matrices))
        return jnp.swapaxes(result, 0, 1)

    load_values = loads.reshape(flat_view).astype(jnp.float32)
    multipliers = apply_jump(lift(coarse_rhs(load_values)))
    start = (load_values - orient_flat * multipliers).astype(jnp.bfloat16)
    residual = apply_jump(module_product(start, pinv_view))
    rho_before = None
    direction = None
    for iteration in range(ITERS):
        projected = project(residual)
        scaled = (orient_flat * projected).astype(jnp.bfloat16)
        smoothed = module_product(scaled, schur_view)
        rho = jnp.sum(scaled.astype(jnp.float32) * smoothed, axis=(1, 2))
        corrected = project(apply_jump(smoothed))
        if iteration == 0:
            direction = corrected
        else:
            direction = corrected + (rho / rho_before)[:, None, None] * direction
        lifted = (orient_flat * direction).astype(jnp.bfloat16)
        response = module_product(lifted, pinv_view)
        kappa = jnp.sum(lifted.astype(jnp.float32) * response, axis=(1, 2))
        stride = rho / kappa
        multipliers = multipliers + stride[:, None, None] * direction
        if iteration + 1 < ITERS:
            residual = residual - stride[:, None, None] * apply_jump(response)
        rho_before = rho
    return multipliers.reshape(case_count, MODULES * NB)
```

```python
import functools

import jax
import jax.numpy as jnp
from jax import lax
from jax.experimental import pallas as pl
from jax.experimental.pallas import tpu as pltpu
from jax.sharding import PartitionSpec as P

MODES = 6
MAXC = 2
ACROSS = 8
BLOCK = 128
LANES = 128
GROUPS = 4
PAD = 8

highest = lax.Precision.HIGHEST
f32 = jnp.float32


def dot(a, b, contract, precision=None):
    return lax.dot_general(a, b, (contract, ((), ())), precision=precision, preferred_element_type=f32)


def exact(a, b, contract):
    return dot(a, b, contract, highest)


def swap_of(group, me):
    if group < 2:
        return (me + group) % 2
    return 2 + (me // ACROSS + group) % 2


def heading_of(swap, me):
    if swap < 2:
        return 1 + (me + swap) % 2
    return 3 + (me // ACROSS + swap) % 2


def swap_routes(count):
    routes = [[], [], [], []]
    for i in range(count):
        for group, offset in enumerate((1, -1, ACROSS, -ACROSS)):
            j = i + offset
            if 0 <= j < count and (group >= 2 or i // ACROSS == j // ACROSS):
                routes[swap_of(group, i)].append((i, j))
    return routes


def block_of(connectors, heading, slot):
    found = jnp.int32(0)
    for b in range(connectors.shape[2]):
        here = (connectors[0, 0, b] == heading) & (connectors[0, 1, b] == slot)
        found = jnp.where(here, b, found)
    return found


def lanes_of(block):
    return pl.ds(pl.multiple_of(block * BLOCK, BLOCK), BLOCK)


def pack_blocks(connectors, me, values, outs):
    for swap, out in enumerate(outs):
        heading = heading_of(swap, me)
        for slot in range(MAXC):
            out[slot] = values[:, lanes_of(block_of(connectors, heading, slot))]


def jump(connectors, me, values, received, out):
    for b in range(connectors.shape[2]):
        heading, slot = connectors[0, 0, b], connectors[0, 1, b]
        lanes = slice(b * BLOCK, (b + 1) * BLOCK)
        out[:, lanes] = jnp.zeros_like(out[:, lanes])
        for group in range(GROUPS):
            for swap in range(2 * (group // 2), 2 * (group // 2) + 2):

                @pl.when((heading == group + 1) & (swap_of(group, me) == swap))
                def _():
                    out[:, lanes] = values[:, lanes] - received[swap][slot]


def send_all(out, piece):
    for device in range(out.shape[0]):
        out[device] = piece


def packed_rows(rows, cases):
    return jnp.concatenate([rows[g * PAD:(g + 1) * PAD] for g in range(GROUPS)], axis=1)


def amplitudes(gathered, coarse, cases):
    flat = gathered[...].reshape(gathered.shape[0] * PAD, GROUPS * cases)
    product = exact(coarse[...], flat, ((1,), (0,)))
    rows = GROUPS * PAD
    total = product[:rows, :cases]
    for g in range(1, GROUPS):
        total = total + product[g * rows:(g + 1) * rows, g * cases:(g + 1) * cases]
    return total


def case_sums(a, b):
    product = a * b
    folded = product[:, :LANES]
    for k in range(1, product.shape[1] // LANES):
        folded = folded + product[:, k * LANES:(k + 1) * LANES]
    return exact(jnp.ones((PAD, LANES), f32), folded, ((1,), (1,)))


def first_kernel(connectors, loads, modes, inverse, mine_out, gather_out, *swap_outs):
    me = lax.axis_index("mod")
    cases = loads.shape[0]
    tiles = mine_out.shape[0]
    rows = exact(modes[...], loads[...].astype(f32), ((1,), (1,)))
    row_id = lax.broadcasted_iota(jnp.int32, (PAD, cases), 0)
    blank = jnp.zeros((PAD, cases), f32)
    padded = jnp.concatenate([rows, jnp.zeros((PAD - MODES, cases), f32)], axis=0)
    pieces = [jnp.where(row_id >= MODES, pltpu.roll(padded, MODES - 2 * g, 0) if g < 3 else blank, blank) for g in range(GROUPS)]
    send_all(gather_out, jnp.concatenate(pieces, axis=1))
    per_tile = LANES // PAD * MODES
    at_row = lax.broadcasted_iota(jnp.int32, (per_tile, LANES), 0)
    at_lane = lax.broadcasted_iota(jnp.int32, (per_tile, LANES), 1)
    spread = ((at_lane % PAD < MODES) & (at_lane // PAD * MODES + at_lane % PAD == at_row)).astype(f32)
    whole = inverse[...]
    for k in range(tiles):
        tile = exact(whole[:, k * per_tile:(k + 1) * per_tile], spread, ((1,), (0,)))
        mine_out[k] = jnp.concatenate([tile, jnp.zeros((PAD - MODES, LANES), f32)], axis=0)
    for swap, out in enumerate(swap_outs):
        heading = heading_of(swap, me)
        out[...] = jnp.zeros_like(out)
        for slot in range(MAXC):
            out[slot, :MODES] = modes[:, lanes_of(block_of(connectors, heading, slot))]
        for k in range(tiles):
            out[MAXC + k] = mine_out[k]


def spread_modes(connectors, me, modes, received, mode_rows):
    own = jnp.concatenate([modes[...], jnp.zeros((PAD - MODES, modes.shape[1]), f32)], axis=0)
    row_id = lax.broadcasted_iota(jnp.int32, (PAD, BLOCK), 0)
    for b in range(connectors.shape[2]):
        heading, slot = connectors[0, 0, b], connectors[0, 1, b]
        lanes = slice(b * BLOCK, (b + 1) * BLOCK)
        for g in range(GROUPS):
            first, second = received[2 * (g // 2)], received[2 * (g // 2) + 1]
            theirs = jnp.where(swap_of(g, me) % 2 == 0, first[slot], second[slot])
            tile = jnp.where(heading == g + 1, -theirs, 0.0)
            if g < 3:
                mine = jnp.where(heading > 0, pltpu.roll(own[:, lanes], MODES - 2 * g, 0), 0.0)
            else:
                mine = jnp.zeros((PAD, BLOCK), f32)
            mode_rows[g * PAD:(g + 1) * PAD, lanes] = jnp.where(row_id < MODES, tile, mine)


def spread_coarse(me, mine, received, offsets, coarse):
    tiles = mine.shape[0]
    width = tiles * LANES
    row_id = lax.broadcasted_iota(jnp.int32, (PAD, width), 0)
    own = jnp.concatenate([mine[k] for k in range(tiles)], axis=1)
    parts = []
    for g in range(GROUPS):
        first, second = received[2 * (g // 2)], received[2 * (g // 2) + 1]
        pick = swap_of(g, me) % 2 == 0
        theirs = jnp.concatenate([jnp.where(pick, first[MAXC + k], second[MAXC + k]) for k in range(tiles)], axis=1)
        ours = pltpu.roll(own, MODES - 2 * g, 0) if g < 3 else jnp.zeros((PAD, width), f32)
        parts.append(jnp.where(row_id < MODES, theirs, ours))
    rows = jnp.concatenate(parts, axis=0)
    total = GROUPS * PAD
    lane = lax.broadcasted_iota(jnp.int32, (total, width), 1) % PAD
    sum_row = lax.broadcasted_iota(jnp.int32, (total, width), 0) == total - 2
    for g in range(GROUPS):
        near = pltpu.roll(rows, (-PAD * offsets[g]) % width, 1)
        if g < 3:
            own_part = pltpu.roll(rows, MODES - 2 * g, 1)
        else:
            own_part = (sum_row & (lane == MODES)).astype(f32)
        value = jnp.where(lane < MODES, near, own_part)
        coarse[g * total:(g + 1) * total] = value


def second_kernel(offsets, connectors, loads, modes, mine, gathered, pinv, r0, r1, r2, r3,
                  coarse, mode_rows, lifted_out, values_out, gather_out, *swap_outs):
    me = lax.axis_index("mod")
    cases = loads.shape[0]
    received = (r0, r1, r2, r3)
    spread_modes(connectors, me, modes, received, mode_rows)
    spread_coarse(me, mine, received, offsets, coarse)
    amplitude = amplitudes(gathered, coarse, cases)
    lifted = exact(amplitude, mode_rows[...], ((0,), (0,)))
    lifted_out[...] = lifted
    start = (loads[...].astype(f32) - lifted).astype(jnp.bfloat16)
    values_out[...] = dot(start, pinv[...], ((1,), (0,)))
    pack_blocks(connectors, me, values_out, swap_outs)
    send_all(gather_out, packed_rows(exact(mode_rows[...], values_out[...], ((1,), (1,))), cases))


def third_kernel(connectors, values, gathered, coarse, mode_rows, schur, r0, r1, r2, r3,
                 values_out, gather_out, s0, s1, s2, s3, field):
    me = lax.axis_index("mod")
    cases = values.shape[0]
    amplitude = amplitudes(gathered, coarse, cases)
    jump(connectors, me, values, (r0, r1, r2, r3), field)
    projected = field[...] - exact(amplitude, mode_rows[...], ((0,), (0,)))
    scaled = projected.astype(jnp.bfloat16)
    values_out[...] = dot(scaled, schur[...], ((1,), (0,)))
    pack_blocks(connectors, me, values_out, (s0, s1, s2, s3))
    smoothed = values_out[...]
    rows = exact(mode_rows[...], smoothed, ((1,), (1,)))
    partial = case_sums(scaled.astype(f32), smoothed)
    row_id = lax.broadcasted_iota(jnp.int32, (PAD, cases), 0)
    last = jnp.where(row_id == MODES, partial, rows[3 * PAD:])
    send_all(gather_out, packed_rows(jnp.concatenate([rows[:3 * PAD], last], axis=0), cases))


def fourth_kernel(connectors, values, gathered, coarse, mode_rows, pinv, r0, r1, r2, r3,
                  corrected_out, rho_out, gather_out, field):
    me = lax.axis_index("mod")
    cases = values.shape[0]
    amplitude = amplitudes(gathered, coarse, cases)
    rho_out[...] = amplitude[3 * PAD:]
    jump(connectors, me, values, (r0, r1, r2, r3), field)
    corrected = field[...] - exact(amplitude, mode_rows[...], ((0,), (0,)))
    corrected_out[...] = corrected
    lifted = corrected.astype(jnp.bfloat16)
    response = dot(lifted, pinv[...], ((1,), (0,)))
    partial = case_sums(lifted.astype(f32), response)
    piece = jnp.concatenate([partial[:1], jnp.zeros((1, LANES - cases), f32)], axis=1)
    send_all(gather_out, piece)


def last_kernel(connectors, gathered, rho, corrected, lifted, out):
    cases = corrected.shape[0]
    kappa = jnp.sum(gathered[...], axis=0)[:, :cases]
    stride = rho[MODES:MODES + 1, :] / kappa
    at_row = lax.broadcasted_iota(jnp.int32, (cases, cases), 0)
    at_lane = lax.broadcasted_iota(jnp.int32, (cases, cases), 1)
    column = jnp.sum(jnp.where(at_row == at_lane, stride, 0.0), axis=1, keepdims=True)
    for b in range(connectors.shape[2]):
        lanes = slice(b * BLOCK, (b + 1) * BLOCK)
        sign = connectors[0, 2, b].astype(f32)
        out[:, lanes] = sign * (lifted[:, lanes] + column * corrected[:, lanes])


def call(kernel, arguments, outs, scratch=()):
    vmem = pl.BlockSpec(memory_space=pltpu.VMEM)
    smem = pl.BlockSpec(memory_space=pltpu.SMEM)
    return pl.pallas_call(
        kernel,
        out_shape=[jax.ShapeDtypeStruct(shape, f32) for shape in outs],
        in_specs=[smem] + [vmem] * (len(arguments) - 1),
        out_specs=[vmem] * len(outs),
        scratch_shapes=list(scratch),
        compiler_params=pltpu.CompilerParams(vmem_limit_bytes=40 * 1024 * 1024),
    )(*arguments)


def on_device(loads, modes, pinv, schur, coarse_inverse, connectors):
    cases, dofs = loads.shape
    count = coarse_inverse.shape[1] // MODES
    tiles = count * PAD // LANES
    routes = swap_routes(count)
    offsets = (1, -1, ACROSS, -ACROSS)
    rows = GROUPS * PAD
    piece = (count, PAD, GROUPS * cases)
    blocks = (MAXC, cases, BLOCK)
    field = (cases, dofs)

    def swapped(packs):
        return [lax.ppermute(pack, "mod", route) for pack, route in zip(packs, routes)]

    def exchanged(pieces):
        return lax.all_to_all(pieces, "mod", 0, 0)

    mine, pieces, *packs = call(
        first_kernel, (connectors, loads, modes, coarse_inverse),
        [(tiles, PAD, LANES), piece] + [(MAXC + tiles, PAD, LANES)] * 4,
    )
    gathered, received = exchanged(pieces), swapped(packs)
    coarse, mode_rows, lifted, values, pieces, *packs = call(
        functools.partial(second_kernel, offsets),
        (connectors, loads, modes, mine, gathered, pinv, *received),
        [(GROUPS * rows, tiles * LANES), (rows, dofs), field, field, piece] + [blocks] * 4,
    )
    gathered, received = exchanged(pieces), swapped(packs)
    values, pieces, *packs = call(
        third_kernel, (connectors, values, gathered, coarse, mode_rows, schur, *received),
        [field, piece] + [blocks] * 4, [pltpu.VMEM(field, f32)],
    )
    gathered, received = exchanged(pieces), swapped(packs)
    corrected, rho, pieces = call(
        fourth_kernel, (connectors, values, gathered, coarse, mode_rows, pinv, *received),
        [field, (PAD, cases), (count, 1, LANES)], [pltpu.VMEM(field, f32)],
    )
    gathered = exchanged(pieces)
    return call(last_kernel, (connectors, gathered, rho, corrected, lifted), [field])[0]


def solution(mesh):
    in_specs = (
        P(None, "mod"),
        P(None, "mod"),
        P("mod", None),
        P("mod", None),
        P("mod", None),
        P("mod", None, None),
    )
    return jax.shard_map(
        on_device, mesh=mesh, in_specs=in_specs, out_specs=P(None, "mod"), check_vma=False
    )
```

```python
import functools

import jax
import jax.numpy as jnp
from jax import lax
from jax.experimental import pallas as pl
from jax.experimental.pallas import tpu as pltpu
from jax.sharding import PartitionSpec as P

MODES = 6
MAXC = 2
ACROSS = 8
BLOCK = 128
LANES = 128
GROUPS = 4
PAD = 8

highest = lax.Precision.HIGHEST
f32 = jnp.float32


def dot(a, b, contract, precision=None):
    return lax.dot_general(a, b, (contract, ((), ())), precision=precision, preferred_element_type=f32)


def exact(a, b, contract):
    return dot(a, b, contract, highest)


def swap_of(group, me):
    if group < 2:
        return (me + group) % 2
    return 2 + (me // ACROSS + group) % 2


def heading_of(swap, me):
    if swap < 2:
        return 1 + (me + swap) % 2
    return 3 + (me // ACROSS + swap) % 2


def swap_routes(count):
    routes = [[], [], [], []]
    for i in range(count):
        for group, offset in enumerate((1, -1, ACROSS, -ACROSS)):
            j = i + offset
            if 0 <= j < count and (group >= 2 or i // ACROSS == j // ACROSS):
                routes[swap_of(group, i)].append((i, j))
    return routes


PLACE = (3, 1, 2, 0)
AHEAD = 2e9


def by_swap(places):
    return [places[PLACE[swap]] for swap in range(GROUPS)]


def block_lanes(b):
    return slice(b * BLOCK, (b + 1) * BLOCK)


def codes_of(table, cases):
    count = table.shape[1] // BLOCK
    return [jnp.broadcast_to(table[MODES:MODES + 1, block_lanes(b)], (cases, BLOCK)) for b in range(count)]


def code_at(heading, slot):
    return jnp.asarray(2 * heading + slot, jnp.int32).astype(f32)


def own_modes(table):
    row_id = lax.broadcasted_iota(jnp.int32, (PAD, table.shape[1]), 0)
    return jnp.where(row_id < MODES, table[:PAD, :], 0.0)


def chosen(values, codes, code):
    found = jnp.zeros_like(values[0])
    for value, mine in zip(values, codes):
        found = jnp.where(mine == code, value, found)
    return found


def pack_blocks(me, codes, values, outs):
    blocks = [values[:, block_lanes(b)] for b in range(len(codes))]
    for swap, out in enumerate(by_swap(outs)):
        for slot in range(MAXC):
            out[slot] = chosen(blocks, codes, code_at(heading_of(swap, me), slot))


def arrived(me, received, at):
    received = by_swap(received)
    pieces = []
    for g in range(GROUPS):
        first, second = received[2 * (g // 2)], received[2 * (g // 2) + 1]
        pieces.append(jnp.where(swap_of(g, me) % 2 == 0, first[at], second[at]))
    return pieces


def jump(me, codes, values, received, out):
    theirs = [arrived(me, received, slot) for slot in range(MAXC)]
    for b, code in enumerate(codes):
        partner = jnp.zeros_like(code)
        for g in range(GROUPS):
            for slot in range(MAXC):
                partner = jnp.where(code == 2 * (g + 1) + slot, theirs[slot][g], partner)
        out[:, block_lanes(b)] = jnp.where(code >= 2, values[:, block_lanes(b)] - partner, 0.0)


def send_all(out, piece):
    for device in range(out.shape[0]):
        out[device] = piece


def packed_rows(rows, cases):
    return jnp.concatenate([rows[g * PAD:(g + 1) * PAD] for g in range(GROUPS)], axis=1)


def amplitudes(gathered, coarse, cases):
    flat = gathered[...].reshape(gathered.shape[0] * PAD, GROUPS * cases)
    product = exact(coarse[...], flat, ((1,), (0,)))
    rows = GROUPS * PAD
    total = product[:rows, :cases]
    for g in range(1, GROUPS):
        total = total + product[g * rows:(g + 1) * rows, g * cases:(g + 1) * cases]
    return total


def case_sums(a, b):
    product = a * b
    folded = product[:, :LANES]
    for k in range(1, product.shape[1] // LANES):
        folded = folded + product[:, k * LANES:(k + 1) * LANES]
    return exact(jnp.ones((PAD, LANES), f32), folded, ((1,), (1,)))


def first_kernel(cases, table, gather_out, s0, s1, s2, s3):
    me = lax.axis_index("mod")
    own = own_modes(table)
    loads_end = PAD + cases
    rows = exact(own, table[PAD:loads_end, :], ((1,), (1,)))
    row_id = lax.broadcasted_iota(jnp.int32, (PAD, cases), 0)
    blank = jnp.zeros((PAD, cases), f32)
    pieces = [jnp.where(row_id >= MODES, pltpu.roll(rows, MODES - 2 * g, 0), blank) for g in range(3)]
    send_all(gather_out, jnp.concatenate(pieces + [blank], axis=1))
    codes = codes_of(table, PAD)
    blocks = [own[:, block_lanes(b)] for b in range(len(codes))]
    per_row = table.shape[1] // LANES
    for swap, out in enumerate(by_swap((s0, s1, s2, s3))):
        for slot in range(MAXC):
            out[slot] = chosen(blocks, codes, code_at(heading_of(swap, me), slot))
        for k in range(out.shape[0] - MAXC):
            top = loads_end + k // per_row * PAD
            out[MAXC + k] = table[top:top + PAD, block_lanes(k % per_row)]


def spread_modes(me, table, received, mode_rows):
    own = own_modes(table)
    row_id = lax.broadcasted_iota(jnp.int32, (PAD, BLOCK), 0)
    theirs = [arrived(me, received, slot) for slot in range(MAXC)]
    shifted = [pltpu.roll(own, MODES - 2 * g, 0) for g in range(3)]
    for b, code in enumerate(codes_of(table, PAD)):
        lanes = block_lanes(b)
        for g in range(GROUPS):
            tile = jnp.zeros((PAD, BLOCK), f32)
            for slot in range(MAXC):
                tile = jnp.where(code == 2 * (g + 1) + slot, -theirs[slot][g], tile)
            mine = jnp.where(code >= 2, shifted[g][:, lanes], 0.0) if g < 3 else jnp.zeros((PAD, BLOCK), f32)
            mode_rows[g * PAD:(g + 1) * PAD, lanes] = jnp.where(row_id < MODES, tile, mine)


def spread_coarse(me, table, cases, received, offsets, coarse):
    raw_tiles = received[0].shape[0] - MAXC
    per_row = table.shape[1] // LANES
    row_id = lax.broadcasted_iota(jnp.int32, (PAD, LANES), 0)
    tiles = []
    for k in range(raw_tiles):
        top = PAD + cases + k // per_row * PAD
        own = table[top:top + PAD, block_lanes(k % per_row)]
        theirs = arrived(me, received, MAXC + k)
        parts = []
        for g in range(GROUPS):
            ours = pltpu.roll(own, MODES - 2 * g, 0) if g < 3 else jnp.zeros((PAD, LANES), f32)
            parts.append(jnp.where(row_id < MODES, theirs[g], ours))
        tiles.append(jnp.concatenate(parts, axis=0))
    raw = jnp.concatenate(tiles, axis=1)
    per_tile = LANES // PAD * MODES
    at_row = lax.broadcasted_iota(jnp.int32, (per_tile, LANES), 0)
    at_lane = lax.broadcasted_iota(jnp.int32, (per_tile, LANES), 1)
    spread = ((at_lane % PAD < MODES) & (at_lane // PAD * MODES + at_lane % PAD == at_row)).astype(f32)
    width = coarse.shape[1]
    rows = jnp.concatenate(
        [exact(raw[:, k * per_tile:(k + 1) * per_tile], spread, ((1,), (0,))) for k in range(width // LANES)], axis=1
    )
    total = GROUPS * PAD
    lane = lax.broadcasted_iota(jnp.int32, (total, width), 1) % PAD
    sum_row = lax.broadcasted_iota(jnp.int32, (total, width), 0) == total - 2
    for g in range(GROUPS):
        near = pltpu.roll(rows, (-PAD * offsets[g]) % width, 1)
        own_part = pltpu.roll(rows, MODES - 2 * g, 1) if g < 3 else (sum_row & (lane == MODES)).astype(f32)
        coarse[g * total:(g + 1) * total] = jnp.where(lane < MODES, near, own_part)


def second_kernel(offsets, table, gathered, pinv, r0, r1, r2, r3, coarse, mode_rows, lifted_out, values_out, gather_out, *swap_outs):
    me = lax.axis_index("mod")
    cases = values_out.shape[0]
    received = (r0, r1, r2, r3)
    spread_modes(me, table, received, mode_rows)
    spread_coarse(me, table, cases, received, offsets, coarse)
    amplitude = amplitudes(gathered, coarse, cases)
    lifted = exact(amplitude, mode_rows[...], ((0,), (0,)))
    lifted_out[...] = lifted
    start = (table[PAD:PAD + cases, :] - lifted).astype(jnp.bfloat16)
    values_out[...] = dot(start, pinv[...], ((1,), (0,)))
    pack_blocks(me, codes_of(table, cases), values_out, swap_outs)
    send_all(gather_out, packed_rows(exact(mode_rows[...], values_out[...], ((1,), (1,))), cases))


def third_kernel(table, values, gathered, coarse, mode_rows, schur, r0, r1, r2, r3, values_out, gather_out, s0, s1, s2, s3, field):
    me = lax.axis_index("mod")
    cases = values.shape[0]
    codes = codes_of(table, cases)
    amplitude = amplitudes(gathered, coarse, cases)
    jump(me, codes, values, (r0, r1, r2, r3), field)
    projected = field[...] - exact(amplitude, mode_rows[...], ((0,), (0,)))
    scaled = projected.astype(jnp.bfloat16)
    values_out[...] = dot(scaled, schur[...], ((1,), (0,)))
    pack_blocks(me, codes, values_out, (s0, s1, s2, s3))
    smoothed = values_out[...]
    rows = exact(mode_rows[...], smoothed, ((1,), (1,)))
    partial = case_sums(scaled.astype(f32), smoothed)
    row_id = lax.broadcasted_iota(jnp.int32, (PAD, cases), 0)
    last = jnp.where(row_id == MODES, partial, rows[3 * PAD:])
    send_all(gather_out, packed_rows(jnp.concatenate([rows[:3 * PAD], last], axis=0), cases))


def fourth_kernel(table, values, gathered, coarse, mode_rows, pinv, r0, r1, r2, r3, corrected_out, rho_out, gather_out, field):
    me = lax.axis_index("mod")
    cases = values.shape[0]
    amplitude = amplitudes(gathered, coarse, cases)
    rho_out[...] = amplitude[3 * PAD:]
    jump(me, codes_of(table, cases), values, (r0, r1, r2, r3), field)
    corrected = field[...] - exact(amplitude, mode_rows[...], ((0,), (0,)))
    corrected_out[...] = corrected
    lifted = corrected.astype(jnp.bfloat16)
    response = dot(lifted, pinv[...], ((1,), (0,)))
    partial = case_sums(lifted.astype(f32), response)
    piece = jnp.concatenate([partial[:1], jnp.zeros((1, LANES - cases), f32)], axis=1)
    send_all(gather_out, piece)


def last_kernel(table, gathered, rho, corrected, lifted, out):
    cases = corrected.shape[0]
    kappa = jnp.sum(gathered[...], axis=0)[:, :cases]
    stride = rho[MODES:MODES + 1, :] / kappa
    at_row = lax.broadcasted_iota(jnp.int32, (cases, cases), 0)
    at_lane = lax.broadcasted_iota(jnp.int32, (cases, cases), 1)
    column = jnp.sum(jnp.where(at_row == at_lane, stride, 0.0), axis=1, keepdims=True)
    out[...] = table[MODES + 1:MODES + 2, :] * (lifted[...] + column * corrected[...])


def call(kernel, arguments, outs, scratch=(), flops=None):
    vmem = pl.BlockSpec(memory_space=pltpu.VMEM)
    cost = None
    if flops:
        cost = pl.CostEstimate(flops=int(flops), bytes_accessed=0, transcendentals=0)
    return pl.pallas_call(
        kernel,
        out_shape=[jax.ShapeDtypeStruct(shape, f32) for shape in outs],
        in_specs=[vmem] * len(arguments),
        out_specs=[vmem] * len(outs),
        scratch_shapes=list(scratch),
        compiler_params=pltpu.CompilerParams(vmem_limit_bytes=24 * 1024 * 1024),
        cost_estimate=cost,
    )(*arguments)


def table_of(loads, modes, coarse_inverse, connectors):
    dofs = loads.shape[1]
    own = connectors[0].astype(f32)
    codes = jnp.stack([2 * own[0] + own[1], own[2]])
    pieces = [modes, jnp.repeat(codes, BLOCK, axis=1), loads.astype(f32)]
    for start in range(0, coarse_inverse.shape[1], dofs):
        part = coarse_inverse[:, start:start + dofs]
        pieces.append(jnp.pad(part, ((0, PAD - MODES), (0, dofs - part.shape[1]))))
    return jnp.concatenate(pieces, axis=0)


def on_device(loads, modes, pinv, schur, coarse_inverse, connectors):
    cases, dofs = loads.shape
    count = coarse_inverse.shape[1] // MODES
    raw_tiles = pl.cdiv(coarse_inverse.shape[1], LANES)
    routes = swap_routes(count)
    offsets = (1, -1, ACROSS, -ACROSS)
    rows = GROUPS * PAD
    piece = (count, PAD, GROUPS * cases)
    blocks = (MAXC, cases, BLOCK)
    field = (cases, dofs)

    def swapped(packs):
        ordered = sorted(range(GROUPS), key=lambda swap: PLACE[swap])
        return [lax.ppermute(pack, "mod", routes[swap]) for pack, swap in zip(packs, ordered)]

    def exchanged(pieces):
        return lax.all_to_all(pieces, "mod", 0, 0)

    table = table_of(loads, modes, coarse_inverse, connectors)
    pieces, *packs = call(
        functools.partial(first_kernel, cases), (table,), [piece] + [(MAXC + raw_tiles, PAD, LANES)] * 4, flops=AHEAD,
    )
    gathered, received = exchanged(pieces), swapped(packs)
    coarse, mode_rows, lifted, values, pieces, *packs = call(
        functools.partial(second_kernel, offsets), (table, gathered, pinv, *received),
        [(GROUPS * rows, count * PAD), (rows, dofs), field, field, piece] + [blocks] * 4,
    )
    gathered, received = exchanged(pieces), swapped(packs)
    values, pieces, *packs = call(
        third_kernel, (table, values, gathered, coarse, mode_rows, schur, *received),
        [field, piece] + [blocks] * 4, [pltpu.VMEM(field, f32)], flops=AHEAD,
    )
    gathered, received = exchanged(pieces), swapped(packs)
    corrected, rho, pieces = call(
        fourth_kernel, (table, values, gathered, coarse, mode_rows, pinv, *received),
        [field, (PAD, cases), (count, 1, LANES)], [pltpu.VMEM(field, f32)],
    )
    gathered = exchanged(pieces)
    return call(last_kernel, (table, gathered, rho, corrected, lifted), [field])[0]


def solution(mesh):
    in_specs = (
        P(None, "mod"),
        P(None, "mod"),
        P("mod", None),
        P("mod", None),
        P("mod", None),
        P("mod", None, None),
    )
    return jax.shard_map(
        on_device, mesh=mesh, in_specs=in_specs, out_specs=P(None, "mod"), check_vma=False
    )
```

```python
import functools

import jax
import jax.numpy as jnp
from jax import lax
from jax.experimental import pallas as pl
from jax.experimental.pallas import tpu as pltpu
from jax.sharding import PartitionSpec as P

MODES = 6
MAXC = 2
ACROSS = 8
BLOCK = 128
LANES = 128
GROUPS = 4
PAD = 8

highest = lax.Precision.HIGHEST
f32 = jnp.float32


def dot(a, b, contract, precision=None):
    return lax.dot_general(a, b, (contract, ((), ())), precision=precision, preferred_element_type=f32)


def exact(a, b, contract):
    return dot(a, b, contract, highest)


def swap_of(group, me):
    if group < 2:
        return (me + group) % 2
    return 2 + (me // ACROSS + group) % 2


def heading_of(swap, me):
    if swap < 2:
        return 1 + (me + swap) % 2
    return 3 + (me // ACROSS + swap) % 2


def swap_routes(count):
    routes = [[], [], [], []]
    for i in range(count):
        for group, offset in enumerate((1, -1, ACROSS, -ACROSS)):
            j = i + offset
            if 0 <= j < count and (group >= 2 or i // ACROSS == j // ACROSS):
                routes[swap_of(group, i)].append((i, j))
    return routes


PLACE = (3, 1, 2, 0)
BANDS = 4
AHEAD = 2e9


def by_swap(places):
    return [places[PLACE[swap]] for swap in range(GROUPS)]


def block_lanes(b):
    return slice(b * BLOCK, (b + 1) * BLOCK)


def inverse_place(tile, cases, dofs):
    per_row = dofs // LANES
    return PAD + cases + tile // per_row * PAD, block_lanes(tile % per_row)


def codes_of(table, cases):
    count = table.shape[1] // BLOCK
    return [jnp.broadcast_to(table[MODES:MODES + 1, block_lanes(b)], (cases, BLOCK)) for b in range(count)]


def code_at(heading, slot):
    return jnp.asarray(2 * heading + slot, jnp.int32).astype(f32)


def own_modes(table):
    row_id = lax.broadcasted_iota(jnp.int32, (PAD, table.shape[1]), 0)
    return jnp.where(row_id < MODES, table[:PAD, :], 0.0)


def chosen(values, codes, code):
    found = jnp.zeros_like(values[0])
    for value, mine in zip(values, codes):
        found = jnp.where(mine == code, value, found)
    return found


def pack_blocks(me, codes, values, outs):
    blocks = [values[:, block_lanes(b)] for b in range(len(codes))]
    for swap, out in enumerate(by_swap(outs)):
        for slot in range(MAXC):
            out[slot] = chosen(blocks, codes, code_at(heading_of(swap, me), slot))


def arrived(me, received, at):
    received = by_swap(received)
    pieces = []
    for g in range(GROUPS):
        first, second = received[2 * (g // 2)], received[2 * (g // 2) + 1]
        pieces.append(jnp.where(swap_of(g, me) % 2 == 0, first[at], second[at]))
    return pieces


def jump(me, codes, values, received, out):
    theirs = [arrived(me, received, slot) for slot in range(MAXC)]
    for b, code in enumerate(codes):
        partner = jnp.zeros_like(code)
        for g in range(GROUPS):
            for slot in range(MAXC):
                partner = jnp.where(code == 2 * (g + 1) + slot, theirs[slot][g], partner)
        out[:, block_lanes(b)] = jnp.where(code >= 2, values[:, block_lanes(b)] - partner, 0.0)


def send_all(out, piece):
    for device in range(out.shape[0]):
        out[device] = piece


def packed_rows(rows, cases):
    return jnp.concatenate([rows[g * PAD:(g + 1) * PAD] for g in range(GROUPS)], axis=1)


def halves(values):
    high = values.astype(jnp.bfloat16)
    return high, (values - high.astype(f32)).astype(jnp.bfloat16)


def amplitudes(gathered, coarse, cases):
    flat = gathered[...].reshape(gathered.shape[0] * PAD, GROUPS * cases)
    wide = GROUPS * cases
    product = dot(coarse[...], jnp.concatenate(halves(flat), axis=1), ((1,), (0,)))
    product = product[:, :wide] + product[:, wide:]
    rows = GROUPS * PAD
    half = GROUPS * rows
    product = product[:half] + product[half:]
    total = product[:rows, :cases]
    for g in range(1, GROUPS):
        total = total + product[g * rows:(g + 1) * rows, g * cases:(g + 1) * cases]
    return total


def lifted_by(amplitude, mode_rows):
    high, low = halves(amplitude)
    return dot(jnp.concatenate([high, high, low, low], axis=0), mode_rows[...], ((0,), (0,)))


def components(rows, values):
    cases = values.shape[0]
    product = dot(rows, jnp.concatenate(halves(values), axis=0), ((1,), (1,)))
    product = product[:, :cases] + product[:, cases:]
    return product[:GROUPS * PAD] + product[GROUPS * PAD:]


def folded(product):
    total = product[:, :LANES]
    for k in range(1, product.shape[1] // LANES):
        total = total + product[:, k * LANES:(k + 1) * LANES]
    return total


def case_sums(fold):
    cases = fold.shape[0]
    at_row = lax.broadcasted_iota(jnp.int32, (cases, cases), 0)
    at_lane = lax.broadcasted_iota(jnp.int32, (cases, cases), 1)
    column = jnp.sum(fold, axis=1, keepdims=True)
    return jnp.sum(jnp.where(at_row == at_lane, column, 0.0), axis=0, keepdims=True)


def first_kernel(connectors_hbm, loads_hbm, modes_hbm, inverse_hbm, table, gather_out, s0, s1, s2, s3,
                 connectors, loads, modes, inverse, pieces, sems, gather_sem):
    me = lax.axis_index("mod")
    cases, dofs = loads.shape
    moves = [
        pltpu.make_async_copy(source, target, sems.at[i])
        for i, (source, target) in enumerate(
            ((loads_hbm, loads), (modes_hbm, modes), (inverse_hbm, inverse), (connectors_hbm, connectors))
        )
    ]
    for move in moves:
        move.start()
    for move in moves:
        move.wait()
    loads_end = PAD + cases
    own = jnp.concatenate([modes[...], jnp.zeros((PAD - MODES, dofs), f32)], axis=0)
    rows = dot(jnp.concatenate(halves(own), axis=0), loads[...], ((1,), (1,)))
    rows = rows[:PAD] + rows[PAD:]
    row_id = lax.broadcasted_iota(jnp.int32, (PAD, cases), 0)
    blank = jnp.zeros((PAD, cases), f32)
    parts = [jnp.where(row_id >= MODES, pltpu.roll(rows, MODES - 2 * g, 0), blank) for g in range(3)]
    send_all(pieces, jnp.concatenate(parts + [blank], axis=1))
    sending = pltpu.make_async_copy(pieces, gather_out, gather_sem)
    sending.start()
    code_row = (2 * connectors[0] + connectors[1]).astype(f32)
    sign_row = connectors[2].astype(f32)
    codes = [jnp.broadcast_to(code_row[:, b:b + 1], (PAD, BLOCK)) for b in range(dofs // BLOCK)]
    blocks = [own[:, block_lanes(b)] for b in range(len(codes))]
    tile_row = lax.broadcasted_iota(jnp.int32, (PAD, BLOCK), 0)
    for b, code in enumerate(codes):
        sign = jnp.broadcast_to(sign_row[:, b:b + 1], (PAD, BLOCK))
        last = jnp.where(tile_row == MODES, code, sign)
        table[:PAD, block_lanes(b)] = jnp.where(tile_row < MODES, blocks[b], last)
    table[PAD:loads_end, :] = loads[...].astype(f32)
    per_tile = LANES // PAD * MODES
    at_row = lax.broadcasted_iota(jnp.int32, (per_tile, LANES), 0)
    at_lane = lax.broadcasted_iota(jnp.int32, (per_tile, LANES), 1)
    spread = ((at_lane % PAD < MODES) & (at_lane // PAD * MODES + at_lane % PAD == at_row)).astype(f32)
    raw = jnp.concatenate([inverse[...], jnp.zeros((PAD - MODES, inverse.shape[1]), f32)], axis=0)
    tiles = [
        exact(raw[:, k * per_tile:(k + 1) * per_tile], spread, ((1,), (0,))) for k in range(s0.shape[0] - MAXC)
    ]
    for k, tile in enumerate(tiles):
        top, lanes = inverse_place(k, cases, dofs)
        table[top:top + PAD, lanes] = tile
    for swap, out in enumerate(by_swap((s0, s1, s2, s3))):
        for slot in range(MAXC):
            out[slot] = chosen(blocks, codes, code_at(heading_of(swap, me), slot))
        for k, tile in enumerate(tiles):
            out[MAXC + k] = tile
    sending.wait()


def spread_modes(me, table, received, rows, mode_rows):
    own = own_modes(table)
    row_id = lax.broadcasted_iota(jnp.int32, (PAD, BLOCK), 0)
    theirs = [arrived(me, received, slot) for slot in range(MAXC)]
    shifted = [pltpu.roll(own, MODES - 2 * g, 0) for g in range(3)]
    for b, code in enumerate(codes_of(table, PAD)):
        lanes = block_lanes(b)
        for g in range(GROUPS):
            tile = jnp.zeros((PAD, BLOCK), f32)
            for slot in range(MAXC):
                tile = jnp.where(code == 2 * (g + 1) + slot, -theirs[slot][g], tile)
            mine = jnp.where(code >= 2, shifted[g][:, lanes], 0.0) if g < 3 else jnp.zeros((PAD, BLOCK), f32)
            rows[g * PAD:(g + 1) * PAD, lanes] = jnp.where(row_id < MODES, tile, mine)
    high, low = halves(rows[...])
    for k, part in enumerate((high, low, high, low)):
        mode_rows[k * GROUPS * PAD:(k + 1) * GROUPS * PAD, :] = part


def spread_coarse(me, table, cases, received, offsets, coarse):
    width = coarse.shape[1]
    row_id = lax.broadcasted_iota(jnp.int32, (PAD, LANES), 0)
    tiles = []
    for k in range(width // LANES):
        top, lanes = inverse_place(k, cases, table.shape[1])
        own = table[top:top + PAD, lanes]
        theirs = arrived(me, received, MAXC + k)
        parts = []
        for g in range(GROUPS):
            ours = pltpu.roll(own, MODES - 2 * g, 0) if g < 3 else jnp.zeros((PAD, LANES), f32)
            parts.append(jnp.where(row_id < MODES, theirs[g], ours))
        tiles.append(jnp.concatenate(parts, axis=0))
    rows = jnp.concatenate(tiles, axis=1)
    total = GROUPS * PAD
    lane = lax.broadcasted_iota(jnp.int32, (total, width), 1) % PAD
    sum_row = lax.broadcasted_iota(jnp.int32, (total, width), 0) == total - 2
    for g in range(GROUPS):
        near = pltpu.roll(rows, (-PAD * offsets[g]) % width, 1)
        own_part = pltpu.roll(rows, MODES - 2 * g, 1) if g < 3 else (sum_row & (lane == MODES)).astype(f32)
        high, low = halves(jnp.where(lane < MODES, near, own_part))
        coarse[g * total:(g + 1) * total] = high
        coarse[(GROUPS + g) * total:(GROUPS + g + 1) * total] = low


def second_kernel(offsets, table, gathered, pinv, r0, r1, r2, r3,
                  coarse, mode_rows, lifted_out, values_out, gather_out, s0, s1, s2, s3, rows, pieces, gather_sem):
    me = lax.axis_index("mod")
    cases = values_out.shape[0]
    received = (r0, r1, r2, r3)
    spread_modes(me, table, received, rows, mode_rows)
    spread_coarse(me, table, cases, received, offsets, coarse)
    amplitude = amplitudes(gathered, coarse, cases)
    lifted = lifted_by(amplitude, mode_rows)
    lifted_out[...] = lifted
    start = (table[PAD:PAD + cases, :] - lifted).astype(jnp.bfloat16)
    values_out[...] = dot(start, pinv[...], ((1,), (0,)))
    send_all(pieces, packed_rows(components(mode_rows[:2 * GROUPS * PAD, :], values_out[...]), cases))
    sending = pltpu.make_async_copy(pieces, gather_out, gather_sem)
    sending.start()
    pack_blocks(me, codes_of(table, cases), values_out, (s0, s1, s2, s3))
    sending.wait()


def third_kernel(table, values, gathered, coarse, mode_rows, schur_hbm, r0, r1, r2, r3,
                 values_out, gather_out, s0, s1, s2, s3, field, schur, pieces, gather_sem, schur_sems):
    parts = schur_sems.shape[0]
    depth = schur.shape[0] // parts
    bands = [slice(i * depth, (i + 1) * depth) for i in range(parts)]
    moves = [
        pltpu.make_async_copy(schur_hbm.at[band, :], schur.at[band, :], schur_sems.at[i]) for i, band in enumerate(bands)
    ]
    for move in moves:
        move.start()
    me = lax.axis_index("mod")
    cases = values.shape[0]
    codes = codes_of(table, cases)
    amplitude = amplitudes(gathered, coarse, cases)
    jump(me, codes, values, (r0, r1, r2, r3), field)
    scaled = (field[...] - lifted_by(amplitude, mode_rows)).astype(jnp.bfloat16)
    smoothed = jnp.zeros(scaled.shape, f32)
    for band, move in zip(bands, moves):
        move.wait()
        smoothed = smoothed + dot(scaled[:, band], schur[band, :], ((1,), (0,)))
    values_out[...] = smoothed
    rows = components(mode_rows[:2 * GROUPS * PAD, :], smoothed)
    partial = folded(scaled.astype(f32) * smoothed)
    row_id = lax.broadcasted_iota(jnp.int32, (PAD, cases), 0)
    last = jnp.where(row_id == MODES, case_sums(partial), rows[3 * PAD:])
    send_all(pieces, packed_rows(jnp.concatenate([rows[:3 * PAD], last], axis=0), cases))
    sending = pltpu.make_async_copy(pieces, gather_out, gather_sem)
    sending.start()
    pack_blocks(me, codes, values_out, (s0, s1, s2, s3))
    sending.wait()


def fourth_kernel(table, values, gathered, coarse, mode_rows, pinv, r0, r1, r2, r3, corrected_out, rho_out, gather_out, field):
    me = lax.axis_index("mod")
    cases = values.shape[0]
    amplitude = amplitudes(gathered, coarse, cases)
    rho_out[...] = amplitude[3 * PAD:]
    jump(me, codes_of(table, cases), values, (r0, r1, r2, r3), field)
    corrected = field[...] - lifted_by(amplitude, mode_rows)
    corrected_out[...] = corrected
    lifted = corrected.astype(jnp.bfloat16)
    response = dot(lifted, pinv[...], ((1,), (0,)))
    partial = case_sums(folded(lifted.astype(f32) * response))
    piece = jnp.concatenate([partial, jnp.zeros((1, LANES - cases), f32)], axis=1)
    send_all(gather_out, piece)


def last_kernel(table, gathered, rho, corrected, lifted, out):
    cases = corrected.shape[0]
    kappa = jnp.sum(gathered[...], axis=0)[:, :cases]
    stride = rho[MODES:MODES + 1, :] / kappa
    at_row = lax.broadcasted_iota(jnp.int32, (cases, cases), 0)
    at_lane = lax.broadcasted_iota(jnp.int32, (cases, cases), 1)
    column = jnp.sum(jnp.where(at_row == at_lane, stride, 0.0), axis=1, keepdims=True)
    out[...] = table[MODES + 1:MODES + 2, :] * (lifted[...] + column * corrected[...])


def call(kernel, arguments, outs, scratch=(), flops=None, in_hbm=(), out_any=()):
    vmem = pl.BlockSpec(memory_space=pltpu.VMEM)
    hbm = pl.BlockSpec(memory_space=pltpu.HBM)
    anywhere = pl.BlockSpec(memory_space=pl.ANY)
    cost = None
    if flops:
        cost = pl.CostEstimate(flops=int(flops), bytes_accessed=0, transcendentals=0)
    arguments = [
        pltpu.with_memory_space_constraint(argument, pltpu.HBM) if i in in_hbm else argument
        for i, argument in enumerate(arguments)
    ]
    outs = [out if isinstance(out, jax.ShapeDtypeStruct) else jax.ShapeDtypeStruct(out, f32) for out in outs]
    return pl.pallas_call(
        kernel,
        out_shape=outs,
        in_specs=[hbm if i in in_hbm else vmem for i in range(len(arguments))],
        out_specs=[anywhere if i in out_any else vmem for i in range(len(outs))],
        scratch_shapes=list(scratch),
        compiler_params=pltpu.CompilerParams(vmem_limit_bytes=24 * 1024 * 1024),
        cost_estimate=cost,
    )(*arguments)


def on_device(loads, modes, pinv, schur, coarse_inverse, connectors):
    cases, dofs = loads.shape
    count = coarse_inverse.shape[1] // MODES
    tiles = count * PAD // LANES
    routes = swap_routes(count)
    offsets = (1, -1, ACROSS, -ACROSS)
    rows = GROUPS * PAD
    piece = (count, PAD, GROUPS * cases)
    blocks = (MAXC, cases, BLOCK)
    field = (cases, dofs)

    def swapped(packs):
        ordered = sorted(range(GROUPS), key=lambda swap: PLACE[swap])
        return [lax.ppermute(pack, "mod", routes[swap]) for pack, swap in zip(packs, ordered)]

    def exchanged(pieces):
        return lax.all_to_all(pieces, "mod", 0, 0)

    dma = pltpu.SemaphoreType.DMA
    pieces_scratch = [pltpu.VMEM(piece, f32), dma]
    table_rows = PAD + cases + pl.cdiv(count * PAD, dofs) * PAD
    flat_connectors = connectors.transpose(1, 0, 2)
    table, pieces, *packs = call(
        first_kernel, (flat_connectors, loads, modes, coarse_inverse),
        [(table_rows, dofs), piece] + [(MAXC + tiles, PAD, LANES)] * 4,
        [pltpu.VMEM(flat_connectors.shape, jnp.int32), pltpu.VMEM(loads.shape, loads.dtype), pltpu.VMEM(modes.shape, f32),
         pltpu.VMEM(coarse_inverse.shape, f32), pltpu.VMEM(piece, f32), dma((4,)), dma],
        flops=AHEAD, in_hbm=(0, 1, 2, 3), out_any=(1,),
    )
    gathered, received = exchanged(pieces), swapped(packs)
    coarse, mode_rows, lifted, values, pieces, *packs = call(
        functools.partial(second_kernel, offsets), (table, gathered, pinv, *received),
        [jax.ShapeDtypeStruct((2 * GROUPS * rows, count * PAD), jnp.bfloat16),
         jax.ShapeDtypeStruct((4 * rows, dofs), jnp.bfloat16), field, field, piece] + [blocks] * 4,
        [pltpu.VMEM((rows, dofs), f32)] + pieces_scratch, out_any=(4,),
    )
    gathered, received = exchanged(pieces), swapped(packs)
    values, pieces, *packs = call(
        third_kernel, (table, values, gathered, coarse, mode_rows, schur, *received),
        [field, piece] + [blocks] * 4,
        [pltpu.VMEM(field, f32), pltpu.VMEM(schur.shape, schur.dtype)] + pieces_scratch + [dma((BANDS,))],
        flops=AHEAD, in_hbm=(5,), out_any=(1,),
    )
    gathered, received = exchanged(pieces), swapped(packs)
    corrected, rho, pieces = call(
        fourth_kernel, (table, values, gathered, coarse, mode_rows, pinv, *received),
        [field, (PAD, cases), (count, 1, LANES)], [pltpu.VMEM(field, f32)],
    )
    gathered = exchanged(pieces)
    return call(last_kernel, (table, gathered, rho, corrected, lifted), [field])[0]


def solution(mesh):
    in_specs = (
        P(None, "mod"),
        P(None, "mod"),
        P("mod", None),
        P("mod", None),
        P("mod", None),
        P("mod", None, None),
    )
    return jax.shard_map(
        on_device, mesh=mesh, in_specs=in_specs, out_specs=P(None, "mod"), check_vma=False
    )
```

```python
import functools

import jax
import jax.numpy as jnp
from jax import lax
from jax.experimental import pallas as pl
from jax.experimental.pallas import tpu as pltpu
from jax.sharding import PartitionSpec as P

MODES = 6
MAXC = 2
ACROSS = 8
BLOCK = 128
LANES = 128
GROUPS = 4
PAD = 8

highest = lax.Precision.HIGHEST
f32 = jnp.float32


def dot(a, b, contract, precision=None):
    return lax.dot_general(a, b, (contract, ((), ())), precision=precision, preferred_element_type=f32)


def exact(a, b, contract):
    return dot(a, b, contract, highest)


def swap_of(group, me):
    if group < 2:
        return (me + group) % 2
    return 2 + (me // ACROSS + group) % 2


def heading_of(swap, me):
    if swap < 2:
        return 1 + (me + swap) % 2
    return 3 + (me // ACROSS + swap) % 2


def swap_routes(count):
    routes = [[], [], [], []]
    for i in range(count):
        for group, offset in enumerate((1, -1, ACROSS, -ACROSS)):
            j = i + offset
            if 0 <= j < count and (group >= 2 or i // ACROSS == j // ACROSS):
                routes[swap_of(group, i)].append((i, j))
    return routes


PLACE = (3, 1, 2, 0)
AHEAD = 2e9


def by_swap(places):
    return [places[PLACE[swap]] for swap in range(GROUPS)]


def block_lanes(b):
    return slice(b * BLOCK, (b + 1) * BLOCK)


def inverse_place(tile, cases, dofs):
    per_row = dofs // LANES
    return PAD + cases + tile // per_row * PAD, block_lanes(tile % per_row)


def codes_of(table, cases):
    count = table.shape[1] // BLOCK
    return [jnp.broadcast_to(table[MODES:MODES + 1, block_lanes(b)], (cases, BLOCK)) for b in range(count)]


def code_at(heading, slot):
    return jnp.asarray(2 * heading + slot, jnp.int32).astype(f32)


def own_modes(table):
    row_id = lax.broadcasted_iota(jnp.int32, (PAD, table.shape[1]), 0)
    return jnp.where(row_id < MODES, table[:PAD, :], 0.0)


def chosen(values, codes, code):
    found = jnp.zeros_like(values[0])
    for value, mine in zip(values, codes):
        found = jnp.where(mine == code, value, found)
    return found


def pack_blocks(me, codes, values, outs):
    blocks = [values[:, block_lanes(b)] for b in range(len(codes))]
    for swap, out in enumerate(by_swap(outs)):
        for slot in range(MAXC):
            out[slot] = chosen(blocks, codes, code_at(heading_of(swap, me), slot))


def arrived(me, received, at):
    received = by_swap(received)
    pieces = []
    for g in range(GROUPS):
        first, second = received[2 * (g // 2)], received[2 * (g // 2) + 1]
        pieces.append(jnp.where(swap_of(g, me) % 2 == 0, first[at], second[at]))
    return pieces


def jump(me, codes, values, received, out):
    theirs = [arrived(me, received, slot) for slot in range(MAXC)]
    for b, code in enumerate(codes):
        partner = jnp.zeros_like(code)
        for g in range(GROUPS):
            for slot in range(MAXC):
                partner = jnp.where(code == 2 * (g + 1) + slot, theirs[slot][g], partner)
        out[:, block_lanes(b)] = jnp.where(code >= 2, values[:, block_lanes(b)] - partner, 0.0)


def send_all(out, piece):
    for device in range(out.shape[0]):
        out[device] = piece


def packed_rows(rows, cases):
    return jnp.concatenate([rows[g * PAD:(g + 1) * PAD] for g in range(GROUPS)], axis=1)


def halves(values):
    high = values.astype(jnp.bfloat16)
    return high, (values - high.astype(f32)).astype(jnp.bfloat16)


def amplitudes(gathered, coarse, cases):
    flat = gathered[...].reshape(gathered.shape[0] * PAD, GROUPS * cases)
    wide = GROUPS * cases
    product = dot(coarse[...], jnp.concatenate(halves(flat), axis=1), ((1,), (0,)))
    product = product[:, :wide] + product[:, wide:]
    rows = GROUPS * PAD
    half = GROUPS * rows
    product = product[:half] + product[half:]
    total = product[:rows, :cases]
    for g in range(1, GROUPS):
        total = total + product[g * rows:(g + 1) * rows, g * cases:(g + 1) * cases]
    return total


def lifted_by(amplitude, mode_rows):
    high, low = halves(amplitude)
    return dot(jnp.concatenate([high, high, low, low], axis=0), mode_rows[...], ((0,), (0,)))


def components(rows, values):
    cases = values.shape[0]
    product = dot(rows, jnp.concatenate(halves(values), axis=0), ((1,), (1,)))
    product = product[:, :cases] + product[:, cases:]
    return product[:GROUPS * PAD] + product[GROUPS * PAD:]


def folded(product):
    total = product[:, :LANES]
    for k in range(1, product.shape[1] // LANES):
        total = total + product[:, k * LANES:(k + 1) * LANES]
    return total


def case_sums(fold):
    cases = fold.shape[0]
    at_row = lax.broadcasted_iota(jnp.int32, (cases, cases), 0)
    at_lane = lax.broadcasted_iota(jnp.int32, (cases, cases), 1)
    column = jnp.sum(fold, axis=1, keepdims=True)
    return jnp.sum(jnp.where(at_row == at_lane, column, 0.0), axis=0, keepdims=True)


def first_kernel(connectors_hbm, loads_hbm, modes_hbm, inverse_hbm, table, gather_out, s0, s1, s2, s3,
                 connectors, loads, modes, inverse, pieces, sems, gather_sem):
    me = lax.axis_index("mod")
    cases, dofs = loads.shape
    moves = [
        pltpu.make_async_copy(source, target, sems.at[i])
        for i, (source, target) in enumerate(
            ((loads_hbm, loads), (modes_hbm, modes), (inverse_hbm, inverse), (connectors_hbm, connectors))
        )
    ]
    for move in moves:
        move.start()
    for move in moves:
        move.wait()
    loads_end = PAD + cases
    own = jnp.concatenate([modes[...], jnp.zeros((PAD - MODES, dofs), f32)], axis=0)
    rows = dot(jnp.concatenate(halves(own), axis=0), loads[...], ((1,), (1,)))
    rows = rows[:PAD] + rows[PAD:]
    row_id = lax.broadcasted_iota(jnp.int32, (PAD, cases), 0)
    blank = jnp.zeros((PAD, cases), f32)
    parts = [jnp.where(row_id >= MODES, pltpu.roll(rows, MODES - 2 * g, 0), blank) for g in range(3)]
    send_all(pieces, jnp.concatenate(parts + [blank], axis=1))
    sending = pltpu.make_async_copy(pieces, gather_out, gather_sem)
    sending.start()
    code_row = (2 * connectors[0] + connectors[1]).astype(f32)
    sign_row = connectors[2].astype(f32)
    codes = [jnp.broadcast_to(code_row[:, b:b + 1], (PAD, BLOCK)) for b in range(dofs // BLOCK)]
    blocks = [own[:, block_lanes(b)] for b in range(len(codes))]
    tile_row = lax.broadcasted_iota(jnp.int32, (PAD, BLOCK), 0)
    for b, code in enumerate(codes):
        sign = jnp.broadcast_to(sign_row[:, b:b + 1], (PAD, BLOCK))
        last = jnp.where(tile_row == MODES, code, sign)
        table[:PAD, block_lanes(b)] = jnp.where(tile_row < MODES, blocks[b], last)
    table[PAD:loads_end, :] = loads[...].astype(f32)
    per_tile = LANES // PAD * MODES
    at_row = lax.broadcasted_iota(jnp.int32, (per_tile, LANES), 0)
    at_lane = lax.broadcasted_iota(jnp.int32, (per_tile, LANES), 1)
    spread = ((at_lane % PAD < MODES) & (at_lane // PAD * MODES + at_lane % PAD == at_row)).astype(f32)
    raw = jnp.concatenate([inverse[...], jnp.zeros((PAD - MODES, inverse.shape[1]), f32)], axis=0)
    tiles = [
        exact(raw[:, k * per_tile:(k + 1) * per_tile], spread, ((1,), (0,))) for k in range(s0.shape[0] - MAXC)
    ]
    for k, tile in enumerate(tiles):
        top, lanes = inverse_place(k, cases, dofs)
        table[top:top + PAD, lanes] = tile
    for swap, out in enumerate(by_swap((s0, s1, s2, s3))):
        for slot in range(MAXC):
            out[slot] = chosen(blocks, codes, code_at(heading_of(swap, me), slot))
        for k, tile in enumerate(tiles):
            out[MAXC + k] = tile
    sending.wait()


def spread_modes(me, table, received, rows, mode_rows):
    own = own_modes(table)
    row_id = lax.broadcasted_iota(jnp.int32, (PAD, BLOCK), 0)
    theirs = [arrived(me, received, slot) for slot in range(MAXC)]
    shifted = [pltpu.roll(own, MODES - 2 * g, 0) for g in range(3)]
    for b, code in enumerate(codes_of(table, PAD)):
        lanes = block_lanes(b)
        for g in range(GROUPS):
            tile = jnp.zeros((PAD, BLOCK), f32)
            for slot in range(MAXC):
                tile = jnp.where(code == 2 * (g + 1) + slot, -theirs[slot][g], tile)
            mine = jnp.where(code >= 2, shifted[g][:, lanes], 0.0) if g < 3 else jnp.zeros((PAD, BLOCK), f32)
            rows[g * PAD:(g + 1) * PAD, lanes] = jnp.where(row_id < MODES, tile, mine)
    high, low = halves(rows[...])
    for k, part in enumerate((high, low, high, low)):
        mode_rows[k * GROUPS * PAD:(k + 1) * GROUPS * PAD, :] = part


def spread_coarse(me, table, cases, received, offsets, coarse):
    width = coarse.shape[1]
    row_id = lax.broadcasted_iota(jnp.int32, (PAD, LANES), 0)
    tiles = []
    for k in range(width // LANES):
        top, lanes = inverse_place(k, cases, table.shape[1])
        own = table[top:top + PAD, lanes]
        theirs = arrived(me, received, MAXC + k)
        parts = []
        for g in range(GROUPS):
            ours = pltpu.roll(own, MODES - 2 * g, 0) if g < 3 else jnp.zeros((PAD, LANES), f32)
            parts.append(jnp.where(row_id < MODES, theirs[g], ours))
        tiles.append(jnp.concatenate(parts, axis=0))
    rows = jnp.concatenate(tiles, axis=1)
    total = GROUPS * PAD
    lane = lax.broadcasted_iota(jnp.int32, (total, width), 1) % PAD
    for g in range(GROUPS):
        near = pltpu.roll(rows, (-PAD * offsets[g]) % width, 1)
        own_part = pltpu.roll(rows, MODES - 2 * g, 1) if g < 3 else jnp.zeros((total, width), f32)
        high, low = halves(jnp.where(lane < MODES, near, own_part))
        coarse[g * total:(g + 1) * total] = high
        coarse[(GROUPS + g) * total:(GROUPS + g + 1) * total] = low


def second_kernel(offsets, table, gathered, pinv, r0, r1, r2, r3,
                  coarse, mode_rows, lifted_out, values_out, gather_out, s0, s1, s2, s3, rows, pieces, gather_sem):
    me = lax.axis_index("mod")
    cases = values_out.shape[0]
    received = (r0, r1, r2, r3)
    spread_modes(me, table, received, rows, mode_rows)
    spread_coarse(me, table, cases, received, offsets, coarse)
    amplitude = amplitudes(gathered, coarse, cases)
    lifted = lifted_by(amplitude, mode_rows)
    lifted_out[...] = lifted
    start = (table[PAD:PAD + cases, :] - lifted).astype(jnp.bfloat16)
    values_out[...] = dot(start, pinv[...], ((1,), (0,)))
    send_all(pieces, packed_rows(components(mode_rows[:2 * GROUPS * PAD, :], values_out[...]), cases))
    sending = pltpu.make_async_copy(pieces, gather_out, gather_sem)
    sending.start()
    pack_blocks(me, codes_of(table, cases), values_out, (s0, s1, s2, s3))
    sending.wait()


def rho_kernel(scaled, smoothed, rho_out):
    rho_out[...] = case_sums(folded(scaled[...].astype(f32) * smoothed[...]))


def lift_kernel(gathered, coarse, mode_rows, lifted):
    lifted[...] = lifted_by(amplitudes(gathered, coarse, lifted.shape[0]), mode_rows)


def third_kernel(table, values, lifted, mode_rows, schur, r0, r1, r2, r3,
                 values_out, scaled_out, gather_out, s0, s1, s2, s3, field, pieces, gather_sem):
    me = lax.axis_index("mod")
    cases = values.shape[0]
    codes = codes_of(table, cases)
    jump(me, codes, values, (r0, r1, r2, r3), field)
    scaled = (field[...] - lifted[...]).astype(jnp.bfloat16)
    scaled_out[...] = scaled
    smoothed = dot(scaled, schur[...], ((1,), (0,)))
    values_out[...] = smoothed
    rows = components(mode_rows[:2 * GROUPS * PAD, :], smoothed)
    send_all(pieces, packed_rows(rows, cases))
    sending = pltpu.make_async_copy(pieces, gather_out, gather_sem)
    sending.start()
    pack_blocks(me, codes, values_out, (s0, s1, s2, s3))
    sending.wait()


def fourth_kernel(table, values, lifted, rho, pinv, r0, r1, r2, r3, corrected_out, gather_out, field):
    me = lax.axis_index("mod")
    cases = values.shape[0]
    jump(me, codes_of(table, cases), values, (r0, r1, r2, r3), field)
    corrected = field[...] - lifted[...]
    corrected_out[...] = corrected
    direction = corrected.astype(jnp.bfloat16)
    response = dot(direction, pinv[...], ((1,), (0,)))
    kappa = case_sums(folded(direction.astype(f32) * response))
    blank = jnp.zeros((1, LANES - 2 * cases), f32)
    send_all(gather_out, jnp.concatenate([kappa, rho[...], blank], axis=1))


def last_kernel(table, gathered, corrected, lifted, out):
    cases = corrected.shape[0]
    sums = jnp.sum(gathered[...], axis=0)
    stride = sums[:, cases:2 * cases] / sums[:, :cases]
    at_row = lax.broadcasted_iota(jnp.int32, (cases, cases), 0)
    at_lane = lax.broadcasted_iota(jnp.int32, (cases, cases), 1)
    column = jnp.sum(jnp.where(at_row == at_lane, stride, 0.0), axis=1, keepdims=True)
    out[...] = table[MODES + 1:MODES + 2, :] * (lifted[...] + column * corrected[...])


def call(kernel, arguments, outs, scratch=(), flops=None, in_hbm=(), out_any=()):
    vmem = pl.BlockSpec(memory_space=pltpu.VMEM)
    hbm = pl.BlockSpec(memory_space=pltpu.HBM)
    anywhere = pl.BlockSpec(memory_space=pl.ANY)
    cost = None
    if flops:
        cost = pl.CostEstimate(flops=int(flops), bytes_accessed=0, transcendentals=0)
    arguments = [
        pltpu.with_memory_space_constraint(argument, pltpu.HBM) if i in in_hbm else argument
        for i, argument in enumerate(arguments)
    ]
    outs = [out if isinstance(out, jax.ShapeDtypeStruct) else jax.ShapeDtypeStruct(out, f32) for out in outs]
    return pl.pallas_call(
        kernel,
        out_shape=outs,
        in_specs=[hbm if i in in_hbm else vmem for i in range(len(arguments))],
        out_specs=[anywhere if i in out_any else vmem for i in range(len(outs))],
        scratch_shapes=list(scratch),
        compiler_params=pltpu.CompilerParams(vmem_limit_bytes=24 * 1024 * 1024),
        cost_estimate=cost,
    )(*arguments)


def on_device(loads, modes, pinv, schur, coarse_inverse, connectors):
    cases, dofs = loads.shape
    count = coarse_inverse.shape[1] // MODES
    tiles = count * PAD // LANES
    routes = swap_routes(count)
    offsets = (1, -1, ACROSS, -ACROSS)
    rows = GROUPS * PAD
    piece = (count, PAD, GROUPS * cases)
    blocks = (MAXC, cases, BLOCK)
    field = (cases, dofs)

    def swapped(packs):
        ordered = sorted(range(GROUPS), key=lambda swap: PLACE[swap])
        return [lax.ppermute(pack, "mod", routes[swap]) for pack, swap in zip(packs, ordered)]

    def exchanged(pieces):
        return lax.all_to_all(pieces, "mod", 0, 0)

    dma = pltpu.SemaphoreType.DMA
    pieces_scratch = [pltpu.VMEM(piece, f32), dma]
    table_rows = PAD + cases + pl.cdiv(count * PAD, dofs) * PAD
    flat_connectors = connectors.transpose(1, 0, 2)
    table, pieces, *packs = call(
        first_kernel, (flat_connectors, loads, modes, coarse_inverse),
        [(table_rows, dofs), piece] + [(MAXC + tiles, PAD, LANES)] * 4,
        [pltpu.VMEM(flat_connectors.shape, jnp.int32), pltpu.VMEM(loads.shape, loads.dtype), pltpu.VMEM(modes.shape, f32),
         pltpu.VMEM(coarse_inverse.shape, f32), pltpu.VMEM(piece, f32), dma((4,)), dma],
        flops=AHEAD, in_hbm=(0, 1, 2, 3), out_any=(1,),
    )
    gathered, received = exchanged(pieces), swapped(packs)
    coarse, mode_rows, lifted, values, pieces, *packs = call(
        functools.partial(second_kernel, offsets), (table, gathered, pinv, *received),
        [jax.ShapeDtypeStruct((2 * GROUPS * rows, count * PAD), jnp.bfloat16),
         jax.ShapeDtypeStruct((4 * rows, dofs), jnp.bfloat16), field, field, piece] + [blocks] * 4,
        [pltpu.VMEM((rows, dofs), f32)] + pieces_scratch, out_any=(4,),
    )
    gathered, received = exchanged(pieces), swapped(packs)
    residual_lift, = call(lift_kernel, (gathered, coarse, mode_rows), [field], flops=AHEAD)
    values, scaled, pieces, *packs = call(
        third_kernel, (table, values, residual_lift, mode_rows, schur, *received),
        [field, jax.ShapeDtypeStruct(field, jnp.bfloat16), piece] + [blocks] * 4,
        [pltpu.VMEM(field, f32)] + pieces_scratch, out_any=(2,),
    )
    gathered, received = exchanged(pieces), swapped(packs)
    rho, = call(rho_kernel, (scaled, values), [(1, cases)])
    smoothed_lift, = call(lift_kernel, (gathered, coarse, mode_rows), [field], flops=AHEAD)
    corrected, pieces = call(
        fourth_kernel, (table, values, smoothed_lift, rho, pinv, *received),
        [field, (count, 1, LANES)], [pltpu.VMEM(field, f32)],
    )
    gathered = exchanged(pieces)
    return call(last_kernel, (table, gathered, corrected, lifted), [field])[0]


def solution(mesh):
    in_specs = (
        P(None, "mod"),
        P(None, "mod"),
        P("mod", None),
        P("mod", None),
        P("mod", None),
        P("mod", None, None),
    )
    return jax.shard_map(
        on_device, mesh=mesh, in_specs=in_specs, out_specs=P(None, "mod"), check_vma=False
    )
```

```python
import functools

import jax
import jax.numpy as jnp
from jax import lax
from jax.experimental import pallas as pl
from jax.experimental.pallas import tpu as pltpu
from jax.sharding import PartitionSpec as P

MODES = 6
MAXC = 2
ACROSS = 8
BLOCK = 128
LANES = 128
GROUPS = 4
PAD = 8

highest = lax.Precision.HIGHEST
f32 = jnp.float32


def dot(a, b, contract, precision=None):
    return lax.dot_general(a, b, (contract, ((), ())), precision=precision, preferred_element_type=f32)


def exact(a, b, contract):
    return dot(a, b, contract, highest)


def swap_of(group, me):
    if group < 2:
        return (me + group) % 2
    return 2 + (me // ACROSS + group) % 2


def heading_of(swap, me):
    if swap < 2:
        return 1 + (me + swap) % 2
    return 3 + (me // ACROSS + swap) % 2


def swap_routes(count):
    routes = [[], [], [], []]
    for i in range(count):
        for group, offset in enumerate((1, -1, ACROSS, -ACROSS)):
            j = i + offset
            if 0 <= j < count and (group >= 2 or i // ACROSS == j // ACROSS):
                routes[swap_of(group, i)].append((i, j))
    return routes


PLACE = (3, 1, 2, 0)
AHEAD = 2e9


def by_swap(places):
    return [places[PLACE[swap]] for swap in range(GROUPS)]


def block_lanes(b):
    return slice(b * BLOCK, (b + 1) * BLOCK)


def inverse_place(tile, cases, dofs):
    per_row = dofs // LANES
    return PAD + cases + tile // per_row * PAD, block_lanes(tile % per_row)


def codes_of(table, cases):
    count = table.shape[1] // BLOCK
    return [jnp.broadcast_to(table[MODES:MODES + 1, block_lanes(b)], (cases, BLOCK)) for b in range(count)]


def code_at(heading, slot):
    return jnp.asarray(2 * heading + slot, jnp.int32).astype(f32)


def own_modes(table):
    row_id = lax.broadcasted_iota(jnp.int32, (PAD, table.shape[1]), 0)
    return jnp.where(row_id < MODES, table[:PAD, :], 0.0)


def chosen(values, codes, code):
    found = jnp.zeros_like(values[0])
    for value, mine in zip(values, codes):
        found = jnp.where(mine == code, value, found)
    return found


def pack_blocks(me, codes, values, outs):
    blocks = [values[:, block_lanes(b)] for b in range(len(codes))]
    for swap, out in enumerate(by_swap(outs)):
        for slot in range(MAXC):
            out[slot] = chosen(blocks, codes, code_at(heading_of(swap, me), slot))


def arrived(me, received, at):
    received = by_swap(received)
    pieces = []
    for g in range(GROUPS):
        first, second = received[2 * (g // 2)], received[2 * (g // 2) + 1]
        pieces.append(jnp.where(swap_of(g, me) % 2 == 0, first[at], second[at]))
    return pieces


def jump(me, codes, values, received, out):
    theirs = [arrived(me, received, slot) for slot in range(MAXC)]
    for b, code in enumerate(codes):
        partner = jnp.zeros_like(code)
        for g in range(GROUPS):
            for slot in range(MAXC):
                partner = jnp.where(code == 2 * (g + 1) + slot, theirs[slot][g], partner)
        out[:, block_lanes(b)] = jnp.where(code >= 2, values[:, block_lanes(b)] - partner, 0.0)


def send_all(out, piece):
    for device in range(out.shape[0]):
        out[device] = piece


def packed_rows(rows, cases):
    return jnp.concatenate([rows[g * PAD:(g + 1) * PAD] for g in range(GROUPS)], axis=1)


def halves(values):
    high = values.astype(jnp.bfloat16)
    return high, (values - high.astype(f32)).astype(jnp.bfloat16)


def amplitudes(gathered, coarse, cases):
    flat = gathered[...].reshape(gathered.shape[0] * PAD, GROUPS * cases)
    wide = GROUPS * cases
    product = dot(coarse[...], jnp.concatenate(halves(flat), axis=1), ((1,), (0,)))
    product = product[:, :wide] + product[:, wide:]
    rows = GROUPS * PAD
    half = GROUPS * rows
    product = product[:half] + product[half:]
    total = product[:rows, :cases]
    for g in range(1, GROUPS):
        total = total + product[g * rows:(g + 1) * rows, g * cases:(g + 1) * cases]
    return total


def first_amplitudes(gathered, rows, cases):
    flat = gathered[...].reshape(gathered.shape[0] * PAD, GROUPS * cases)[:, :cases]
    product = dot(jnp.concatenate(halves(rows), axis=0), jnp.concatenate(halves(flat), axis=1), ((1,), (0,)))
    product = product[:, :cases] + product[:, cases:]
    return product[:GROUPS * PAD] + product[GROUPS * PAD:]


def lifted_by(amplitude, mode_rows):
    high, low = halves(amplitude)
    cases = amplitude.shape[1]
    left = jnp.concatenate([jnp.concatenate([high, high], axis=0), jnp.concatenate([low, low], axis=0)], axis=1)
    product = dot(left, mode_rows[...], ((0,), (0,)))
    return product[:cases] + product[cases:]


def components(rows, values):
    cases = values.shape[0]
    product = dot(rows, jnp.concatenate(halves(values), axis=0), ((1,), (1,)))
    product = product[:, :cases] + product[:, cases:]
    return product[:GROUPS * PAD] + product[GROUPS * PAD:]


def folded(product):
    total = product[:, :LANES]
    for k in range(1, product.shape[1] // LANES):
        total = total + product[:, k * LANES:(k + 1) * LANES]
    return total


def case_sums(fold):
    cases = fold.shape[0]
    at_row = lax.broadcasted_iota(jnp.int32, (cases, cases), 0)
    at_lane = lax.broadcasted_iota(jnp.int32, (cases, cases), 1)
    column = jnp.sum(fold, axis=1, keepdims=True)
    return jnp.sum(jnp.where(at_row == at_lane, column, 0.0), axis=0, keepdims=True)


def first_kernel(connectors_hbm, loads_hbm, modes_hbm, inverse_hbm, table, gather_out, s0, s1, s2, s3,
                 connectors, loads, modes, inverse, pieces, sems, gather_sem):
    me = lax.axis_index("mod")
    cases, dofs = loads.shape
    moves = [
        pltpu.make_async_copy(source, target, sems.at[i])
        for i, (source, target) in enumerate(
            ((loads_hbm, loads), (modes_hbm, modes), (inverse_hbm, inverse), (connectors_hbm, connectors))
        )
    ]
    for move in moves:
        move.start()
    for move in moves:
        move.wait()
    loads_end = PAD + cases
    own = jnp.concatenate([modes[...], jnp.zeros((PAD - MODES, dofs), f32)], axis=0)
    rows = dot(jnp.concatenate(halves(own), axis=0), loads[...], ((1,), (1,)))
    rows = rows[:PAD] + rows[PAD:]
    send_all(pieces, jnp.concatenate([rows, jnp.zeros((PAD, (GROUPS - 1) * cases), f32)], axis=1))
    sending = pltpu.make_async_copy(pieces, gather_out, gather_sem)
    sending.start()
    code_row = (2 * connectors[0] + connectors[1]).astype(f32)
    sign_row = connectors[2].astype(f32)
    codes = [jnp.broadcast_to(code_row[:, b:b + 1], (PAD, BLOCK)) for b in range(dofs // BLOCK)]
    blocks = [own[:, block_lanes(b)] for b in range(len(codes))]
    tile_row = lax.broadcasted_iota(jnp.int32, (PAD, BLOCK), 0)
    for b, code in enumerate(codes):
        sign = jnp.broadcast_to(sign_row[:, b:b + 1], (PAD, BLOCK))
        last = jnp.where(tile_row == MODES, code, sign)
        table[:PAD, block_lanes(b)] = jnp.where(tile_row < MODES, blocks[b], last)
    table[PAD:loads_end, :] = loads[...].astype(f32)
    per_tile = LANES // PAD * MODES
    at_row = lax.broadcasted_iota(jnp.int32, (per_tile, LANES), 0)
    at_lane = lax.broadcasted_iota(jnp.int32, (per_tile, LANES), 1)
    spread = ((at_lane % PAD < MODES) & (at_lane // PAD * MODES + at_lane % PAD == at_row)).astype(f32)
    raw = jnp.concatenate([inverse[...], jnp.zeros((PAD - MODES, inverse.shape[1]), f32)], axis=0)
    tiles = [
        exact(raw[:, k * per_tile:(k + 1) * per_tile], spread, ((1,), (0,))) for k in range(s0.shape[0] - MAXC)
    ]
    for k, tile in enumerate(tiles):
        top, lanes = inverse_place(k, cases, dofs)
        table[top:top + PAD, lanes] = tile
    for swap, out in enumerate(by_swap((s0, s1, s2, s3))):
        for slot in range(MAXC):
            out[slot] = chosen(blocks, codes, code_at(heading_of(swap, me), slot))
        for k, tile in enumerate(tiles):
            out[MAXC + k] = tile
    sending.wait()


def spread_modes(me, table, received, rows, mode_rows):
    own = own_modes(table)
    row_id = lax.broadcasted_iota(jnp.int32, (PAD, BLOCK), 0)
    theirs = [arrived(me, received, slot) for slot in range(MAXC)]
    shifted = [pltpu.roll(own, MODES - 2 * g, 0) for g in range(3)]
    for b, code in enumerate(codes_of(table, PAD)):
        lanes = block_lanes(b)
        for g in range(GROUPS):
            tile = jnp.zeros((PAD, BLOCK), f32)
            for slot in range(MAXC):
                tile = jnp.where(code == 2 * (g + 1) + slot, -theirs[slot][g], tile)
            mine = jnp.where(code >= 2, shifted[g][:, lanes], 0.0) if g < 3 else jnp.zeros((PAD, BLOCK), f32)
            rows[g * PAD:(g + 1) * PAD, lanes] = jnp.where(row_id < MODES, tile, mine)
    high, low = halves(rows[...])
    for k, part in enumerate((high, low)):
        mode_rows[k * GROUPS * PAD:(k + 1) * GROUPS * PAD, :] = part


def coarse_rows_of(me, table, cases, received, tiles):
    row_id = lax.broadcasted_iota(jnp.int32, (PAD, LANES), 0)
    rows = []
    for k in range(tiles):
        top, lanes = inverse_place(k, cases, table.shape[1])
        own = table[top:top + PAD, lanes]
        theirs = arrived(me, received, MAXC + k)
        parts = []
        for g in range(GROUPS):
            ours = pltpu.roll(own, MODES - 2 * g, 0) if g < 3 else jnp.zeros((PAD, LANES), f32)
            parts.append(jnp.where(row_id < MODES, theirs[g], ours))
        rows.append(jnp.concatenate(parts, axis=0))
    return jnp.concatenate(rows, axis=1)


def spread_coarse(rows, offsets, coarse):
    total, width = rows.shape
    lane = lax.broadcasted_iota(jnp.int32, (total, width), 1) % PAD
    for g in range(GROUPS):
        near = pltpu.roll(rows, (-PAD * offsets[g]) % width, 1)
        own_part = pltpu.roll(rows, MODES - 2 * g, 1) if g < 3 else jnp.zeros((total, width), f32)
        high, low = halves(jnp.where(lane < MODES, near, own_part))
        coarse[g * total:(g + 1) * total] = high
        coarse[(GROUPS + g) * total:(GROUPS + g + 1) * total] = low


def second_kernel(table, gathered, pinv, r0, r1, r2, r3,
                  coarse_rows, mode_rows, lifted_out, values_out, gather_out, s0, s1, s2, s3, rows, pieces, gather_sem):
    me = lax.axis_index("mod")
    cases = values_out.shape[0]
    received = (r0, r1, r2, r3)
    spread_modes(me, table, received, rows, mode_rows)
    coarse_rows[...] = coarse_rows_of(me, table, cases, received, coarse_rows.shape[1] // LANES)
    amplitude = first_amplitudes(gathered, coarse_rows[...], cases)
    lifted = lifted_by(amplitude, mode_rows)
    lifted_out[...] = lifted
    start = (table[PAD:PAD + cases, :] - lifted).astype(jnp.bfloat16)
    values_out[...] = dot(start, pinv[...], ((1,), (0,)))
    send_all(pieces, packed_rows(components(mode_rows[...], values_out[...]), cases))
    sending = pltpu.make_async_copy(pieces, gather_out, gather_sem)
    sending.start()
    pack_blocks(me, codes_of(table, cases), values_out, (s0, s1, s2, s3))
    sending.wait()


def rho_kernel(scaled, smoothed, rho_out):
    rho_out[...] = case_sums(folded(scaled[...].astype(f32) * smoothed[...]))


def first_lift_kernel(offsets, gathered, coarse_rows, mode_rows, lifted, coarse):
    spread_coarse(coarse_rows[...], offsets, coarse)
    lifted[...] = lifted_by(amplitudes(gathered, coarse, lifted.shape[0]), mode_rows)


def lift_kernel(gathered, coarse, mode_rows, lifted):
    lifted[...] = lifted_by(amplitudes(gathered, coarse, lifted.shape[0]), mode_rows)


def third_kernel(table, values, lifted, mode_rows, schur, r0, r1, r2, r3,
                 values_out, scaled_out, gather_out, s0, s1, s2, s3, field, pieces, gather_sem):
    me = lax.axis_index("mod")
    cases = values.shape[0]
    codes = codes_of(table, cases)
    jump(me, codes, values, (r0, r1, r2, r3), field)
    scaled = (field[...] - lifted[...]).astype(jnp.bfloat16)
    scaled_out[...] = scaled
    smoothed = dot(scaled, schur[...], ((1,), (0,)))
    values_out[...] = smoothed
    rows = components(mode_rows[...], smoothed)
    send_all(pieces, packed_rows(rows, cases))
    sending = pltpu.make_async_copy(pieces, gather_out, gather_sem)
    sending.start()
    pack_blocks(me, codes, values_out, (s0, s1, s2, s3))
    sending.wait()


def fourth_kernel(table, values, lifted, rho, pinv, r0, r1, r2, r3, corrected_out, gather_out, field):
    me = lax.axis_index("mod")
    cases = values.shape[0]
    jump(me, codes_of(table, cases), values, (r0, r1, r2, r3), field)
    corrected = field[...] - lifted[...]
    corrected_out[...] = corrected
    direction = corrected.astype(jnp.bfloat16)
    response = dot(direction, pinv[...], ((1,), (0,)))
    kappa = case_sums(folded(direction.astype(f32) * response))
    blank = jnp.zeros((1, LANES - 2 * cases), f32)
    send_all(gather_out, jnp.concatenate([kappa, rho[...], blank], axis=1))


def last_kernel(table, gathered, corrected, lifted, out):
    cases = corrected.shape[0]
    sums = jnp.sum(gathered[...], axis=0)
    stride = sums[:, cases:2 * cases] / sums[:, :cases]
    at_row = lax.broadcasted_iota(jnp.int32, (cases, cases), 0)
    at_lane = lax.broadcasted_iota(jnp.int32, (cases, cases), 1)
    column = jnp.sum(jnp.where(at_row == at_lane, stride, 0.0), axis=1, keepdims=True)
    out[...] = table[MODES + 1:MODES + 2, :] * (lifted[...] + column * corrected[...])


def call(kernel, arguments, outs, scratch=(), flops=None, in_hbm=(), out_any=()):
    vmem = pl.BlockSpec(memory_space=pltpu.VMEM)
    hbm = pl.BlockSpec(memory_space=pltpu.HBM)
    anywhere = pl.BlockSpec(memory_space=pl.ANY)
    cost = None
    if flops:
        cost = pl.CostEstimate(flops=int(flops), bytes_accessed=0, transcendentals=0)
    arguments = [
        pltpu.with_memory_space_constraint(argument, pltpu.HBM) if i in in_hbm else argument
        for i, argument in enumerate(arguments)
    ]
    outs = [out if isinstance(out, jax.ShapeDtypeStruct) else jax.ShapeDtypeStruct(out, f32) for out in outs]
    return pl.pallas_call(
        kernel,
        out_shape=outs,
        in_specs=[hbm if i in in_hbm else vmem for i in range(len(arguments))],
        out_specs=[anywhere if i in out_any else vmem for i in range(len(outs))],
        scratch_shapes=list(scratch),
        compiler_params=pltpu.CompilerParams(vmem_limit_bytes=24 * 1024 * 1024),
        cost_estimate=cost,
    )(*arguments)


def on_device(loads, modes, pinv, schur, coarse_inverse, connectors):
    cases, dofs = loads.shape
    count = coarse_inverse.shape[1] // MODES
    tiles = count * PAD // LANES
    routes = swap_routes(count)
    offsets = (1, -1, ACROSS, -ACROSS)
    rows = GROUPS * PAD
    piece = (count, PAD, GROUPS * cases)
    blocks = (MAXC, cases, BLOCK)
    field = (cases, dofs)

    def swapped(packs):
        ordered = sorted(range(GROUPS), key=lambda swap: PLACE[swap])
        return [lax.ppermute(pack, "mod", routes[swap]) for pack, swap in zip(packs, ordered)]

    def exchanged(pieces):
        return lax.all_to_all(pieces, "mod", 0, 0)

    dma = pltpu.SemaphoreType.DMA
    pieces_scratch = [pltpu.VMEM(piece, f32), dma]
    table_rows = PAD + cases + pl.cdiv(count * PAD, dofs) * PAD
    flat_connectors = connectors.transpose(1, 0, 2)
    table, pieces, *packs = call(
        first_kernel, (flat_connectors, loads, modes, coarse_inverse),
        [(table_rows, dofs), piece] + [(MAXC + tiles, PAD, LANES)] * 4,
        [pltpu.VMEM(flat_connectors.shape, jnp.int32), pltpu.VMEM(loads.shape, loads.dtype), pltpu.VMEM(modes.shape, f32),
         pltpu.VMEM(coarse_inverse.shape, f32), pltpu.VMEM(piece, f32), dma((4,)), dma],
        flops=AHEAD, in_hbm=(0, 1, 2, 3), out_any=(1,),
    )
    gathered, received = exchanged(pieces), swapped(packs)
    coarse_rows, mode_rows, lifted, values, pieces, *packs = call(
        second_kernel, (table, gathered, pinv, *received),
        [(rows, count * PAD),
         jax.ShapeDtypeStruct((2 * rows, dofs), jnp.bfloat16), field, field, piece] + [blocks] * 4,
        [pltpu.VMEM((rows, dofs), f32)] + pieces_scratch, out_any=(4,),
    )
    gathered, received = exchanged(pieces), swapped(packs)
    residual_lift, coarse = call(
        functools.partial(first_lift_kernel, offsets), (gathered, coarse_rows, mode_rows),
        [field, jax.ShapeDtypeStruct((2 * GROUPS * rows, count * PAD), jnp.bfloat16)], flops=AHEAD,
    )
    values, scaled, pieces, *packs = call(
        third_kernel, (table, values, residual_lift, mode_rows, schur, *received),
        [field, jax.ShapeDtypeStruct(field, jnp.bfloat16), piece] + [blocks] * 4,
        [pltpu.VMEM(field, f32)] + pieces_scratch, out_any=(2,),
    )
    gathered, received = exchanged(pieces), swapped(packs)
    rho, = call(rho_kernel, (scaled, values), [(1, cases)])
    smoothed_lift, = call(lift_kernel, (gathered, coarse, mode_rows), [field], flops=AHEAD)
    corrected, pieces = call(
        fourth_kernel, (table, values, smoothed_lift, rho, pinv, *received),
        [field, (count, 1, LANES)], [pltpu.VMEM(field, f32)],
    )
    gathered = exchanged(pieces)
    return call(last_kernel, (table, gathered, corrected, lifted), [field])[0]


def solution(mesh):
    in_specs = (
        P(None, "mod"),
        P(None, "mod"),
        P("mod", None),
        P("mod", None),
        P("mod", None),
        P("mod", None, None),
    )
    return jax.shard_map(
        on_device, mesh=mesh, in_specs=in_specs, out_specs=P(None, "mod"), check_vma=False
    )
```

```python
import functools

import jax
import jax.numpy as jnp
from jax import lax
from jax.experimental import pallas as pl
from jax.experimental.pallas import tpu as pltpu
from jax.sharding import PartitionSpec as P

MODES = 6
MAXC = 2
ACROSS = 8
BLOCK = 128
LANES = 128
GROUPS = 4
PAD = 8

highest = lax.Precision.HIGHEST
f32 = jnp.float32


def dot(a, b, contract, precision=None):
    return lax.dot_general(a, b, (contract, ((), ())), precision=precision, preferred_element_type=f32)


def exact(a, b, contract):
    return dot(a, b, contract, highest)


def swap_of(group, me):
    if group < 2:
        return (me + group) % 2
    return 2 + (me // ACROSS + group) % 2


def heading_of(swap, me):
    if swap < 2:
        return 1 + (me + swap) % 2
    return 3 + (me // ACROSS + swap) % 2


def swap_routes(count):
    routes = [[], [], [], []]
    for i in range(count):
        for group, offset in enumerate((1, -1, ACROSS, -ACROSS)):
            j = i + offset
            if 0 <= j < count and (group >= 2 or i // ACROSS == j // ACROSS):
                routes[swap_of(group, i)].append((i, j))
    return routes


PLACE = (3, 1, 2, 0)
AHEAD = 2e9


def by_swap(places):
    return [places[PLACE[swap]] for swap in range(GROUPS)]


def block_lanes(b):
    return slice(b * BLOCK, (b + 1) * BLOCK)


def inverse_place(tile, cases, dofs):
    per_row = dofs // LANES
    return PAD + cases + tile // per_row * PAD, block_lanes(tile % per_row)


def codes_of(table, cases):
    count = table.shape[1] // BLOCK
    return [jnp.broadcast_to(table[MODES:MODES + 1, block_lanes(b)], (cases, BLOCK)) for b in range(count)]


def code_at(heading, slot):
    return jnp.asarray(2 * heading + slot, jnp.int32).astype(f32)


def own_modes(table):
    row_id = lax.broadcasted_iota(jnp.int32, (PAD, table.shape[1]), 0)
    return jnp.where(row_id < MODES, table[:PAD, :], 0.0)


def chosen(values, codes, code):
    found = jnp.zeros_like(values[0])
    for value, mine in zip(values, codes):
        found = jnp.where(mine == code, value, found)
    return found


def pack_blocks(me, codes, values, outs):
    blocks = [values[:, block_lanes(b)] for b in range(len(codes))]
    for swap, out in enumerate(by_swap(outs)):
        for slot in range(MAXC):
            out[slot] = chosen(blocks, codes, code_at(heading_of(swap, me), slot))


def arrived(me, received, at):
    received = by_swap(received)
    pieces = []
    for g in range(GROUPS):
        first, second = received[2 * (g // 2)], received[2 * (g // 2) + 1]
        pieces.append(jnp.where(swap_of(g, me) % 2 == 0, first[at], second[at]))
    return pieces


def jump(me, codes, values, received, out):
    theirs = [arrived(me, received, slot) for slot in range(MAXC)]
    for b, code in enumerate(codes):
        partner = jnp.zeros_like(code)
        for g in range(GROUPS):
            for slot in range(MAXC):
                partner = jnp.where(code == 2 * (g + 1) + slot, theirs[slot][g], partner)
        out[:, block_lanes(b)] = jnp.where(code >= 2, values[:, block_lanes(b)] - partner, 0.0)


def send_all(out, piece):
    for device in range(out.shape[0]):
        out[device] = piece


def packed_rows(rows, cases):
    return jnp.concatenate([rows[g * PAD:(g + 1) * PAD] for g in range(GROUPS)], axis=1)


def halves(values):
    high = values.astype(jnp.bfloat16)
    return high, (values - high.astype(f32)).astype(jnp.bfloat16)


def amplitudes(gathered, coarse, cases):
    flat = gathered[...].reshape(gathered.shape[0] * PAD, GROUPS * cases)
    wide = GROUPS * cases
    product = dot(coarse[...], jnp.concatenate(halves(flat), axis=1), ((1,), (0,)))
    product = product[:, :wide] + product[:, wide:]
    rows = GROUPS * PAD
    half = GROUPS * rows
    product = product[:half] + product[half:]
    total = product[:rows, :cases]
    for g in range(1, GROUPS):
        total = total + product[g * rows:(g + 1) * rows, g * cases:(g + 1) * cases]
    return total


def first_amplitudes(gathered, rows, cases):
    flat = gathered[...].reshape(gathered.shape[0] * PAD, GROUPS * cases)[:, :cases]
    product = dot(jnp.concatenate(halves(rows), axis=0), jnp.concatenate(halves(flat), axis=1), ((1,), (0,)))
    product = product[:, :cases] + product[:, cases:]
    return product[:GROUPS * PAD] + product[GROUPS * PAD:]


def lifted_by(amplitude, mode_rows):
    high, low = halves(amplitude)
    cases = amplitude.shape[1]
    left = jnp.concatenate([jnp.concatenate([high, high], axis=0), jnp.concatenate([low, low], axis=0)], axis=1)
    product = dot(left, mode_rows[...], ((0,), (0,)))
    return product[:cases] + product[cases:]


def components(rows, values):
    cases = values.shape[0]
    product = dot(rows, jnp.concatenate(halves(values), axis=0), ((1,), (1,)))
    product = product[:, :cases] + product[:, cases:]
    return product[:GROUPS * PAD] + product[GROUPS * PAD:]


def folded(product):
    total = product[:, :LANES]
    for k in range(1, product.shape[1] // LANES):
        total = total + product[:, k * LANES:(k + 1) * LANES]
    return total


def case_sums(fold):
    cases = fold.shape[0]
    at_row = lax.broadcasted_iota(jnp.int32, (cases, cases), 0)
    at_lane = lax.broadcasted_iota(jnp.int32, (cases, cases), 1)
    column = jnp.sum(fold, axis=1, keepdims=True)
    return jnp.sum(jnp.where(at_row == at_lane, column, 0.0), axis=0, keepdims=True)


def first_kernel(connectors_hbm, loads_hbm, modes_hbm, inverse_hbm, table, gather_out, s0, s1, s2, s3,
                 connectors, loads, modes, inverse, pieces, sems, gather_sem):
    me = lax.axis_index("mod")
    cases, dofs = loads.shape
    moves = [
        pltpu.make_async_copy(source, target, sems.at[i])
        for i, (source, target) in enumerate(
            ((loads_hbm, loads), (modes_hbm, modes), (inverse_hbm, inverse), (connectors_hbm, connectors))
        )
    ]
    for move in moves:
        move.start()
    for move in moves:
        move.wait()
    loads_end = PAD + cases
    own = jnp.concatenate([modes[...], jnp.zeros((PAD - MODES, dofs), f32)], axis=0)
    rows = dot(jnp.concatenate(halves(own), axis=0), loads[...], ((1,), (1,)))
    rows = rows[:PAD] + rows[PAD:]
    send_all(pieces, jnp.concatenate([rows, jnp.zeros((PAD, (GROUPS - 1) * cases), f32)], axis=1))
    sending = pltpu.make_async_copy(pieces, gather_out, gather_sem)
    sending.start()
    code_row = (2 * connectors[0] + connectors[1]).astype(f32)
    sign_row = connectors[2].astype(f32)
    codes = [jnp.broadcast_to(code_row[:, b:b + 1], (PAD, BLOCK)) for b in range(dofs // BLOCK)]
    blocks = [own[:, block_lanes(b)] for b in range(len(codes))]
    tile_row = lax.broadcasted_iota(jnp.int32, (PAD, BLOCK), 0)
    for b, code in enumerate(codes):
        sign = jnp.broadcast_to(sign_row[:, b:b + 1], (PAD, BLOCK))
        last = jnp.where(tile_row == MODES, code, sign)
        table[:PAD, block_lanes(b)] = jnp.where(tile_row < MODES, blocks[b], last)
    table[PAD:loads_end, :] = loads[...].astype(f32)
    per_tile = LANES // PAD * MODES
    at_row = lax.broadcasted_iota(jnp.int32, (per_tile, LANES), 0)
    at_lane = lax.broadcasted_iota(jnp.int32, (per_tile, LANES), 1)
    spread = ((at_lane % PAD < MODES) & (at_lane // PAD * MODES + at_lane % PAD == at_row)).astype(f32)
    raw = jnp.concatenate([inverse[...], jnp.zeros((PAD - MODES, inverse.shape[1]), f32)], axis=0)
    tiles = [
        exact(raw[:, k * per_tile:(k + 1) * per_tile], spread, ((1,), (0,))) for k in range(s0.shape[0] - MAXC)
    ]
    for k, tile in enumerate(tiles):
        top, lanes = inverse_place(k, cases, dofs)
        table[top:top + PAD, lanes] = tile
    for swap, out in enumerate(by_swap((s0, s1, s2, s3))):
        for slot in range(MAXC):
            out[slot] = chosen(blocks, codes, code_at(heading_of(swap, me), slot))
        for k, tile in enumerate(tiles):
            out[MAXC + k] = tile
    sending.wait()


def spread_modes(me, table, received, rows, mode_rows):
    own = own_modes(table)
    row_id = lax.broadcasted_iota(jnp.int32, (PAD, BLOCK), 0)
    theirs = [arrived(me, received, slot) for slot in range(MAXC)]
    shifted = [pltpu.roll(own, MODES - 2 * g, 0) for g in range(3)]
    for b, code in enumerate(codes_of(table, PAD)):
        lanes = block_lanes(b)
        for g in range(GROUPS):
            tile = jnp.zeros((PAD, BLOCK), f32)
            for slot in range(MAXC):
                tile = jnp.where(code == 2 * (g + 1) + slot, -theirs[slot][g], tile)
            mine = jnp.where(code >= 2, shifted[g][:, lanes], 0.0) if g < 3 else jnp.zeros((PAD, BLOCK), f32)
            rows[g * PAD:(g + 1) * PAD, lanes] = jnp.where(row_id < MODES, tile, mine)
    high, low = halves(rows[...])
    for k, part in enumerate((high, low)):
        mode_rows[k * GROUPS * PAD:(k + 1) * GROUPS * PAD, :] = part


def coarse_rows_of(me, table, cases, received, tiles):
    row_id = lax.broadcasted_iota(jnp.int32, (PAD, LANES), 0)
    rows = []
    for k in range(tiles):
        top, lanes = inverse_place(k, cases, table.shape[1])
        own = table[top:top + PAD, lanes]
        theirs = arrived(me, received, MAXC + k)
        parts = []
        for g in range(GROUPS):
            ours = pltpu.roll(own, MODES - 2 * g, 0) if g < 3 else jnp.zeros((PAD, LANES), f32)
            parts.append(jnp.where(row_id < MODES, theirs[g], ours))
        rows.append(jnp.concatenate(parts, axis=0))
    return jnp.concatenate(rows, axis=1)


def spread_coarse(rows, offsets, coarse):
    total, width = rows.shape
    lane = lax.broadcasted_iota(jnp.int32, (total, width), 1) % PAD
    for g in range(GROUPS):
        near = pltpu.roll(rows, (-PAD * offsets[g]) % width, 1)
        own_part = pltpu.roll(rows, MODES - 2 * g, 1) if g < 3 else jnp.zeros((total, width), f32)
        high, low = halves(jnp.where(lane < MODES, near, own_part))
        coarse[g * total:(g + 1) * total] = high
        coarse[(GROUPS + g) * total:(GROUPS + g + 1) * total] = low


def second_kernel(table, gathered, pinv, r0, r1, r2, r3,
                  coarse_rows, mode_rows, lifted_out, values_out, gather_out, s0, s1, s2, s3, rows, pieces, gather_sem):
    me = lax.axis_index("mod")
    cases = values_out.shape[0]
    received = (r0, r1, r2, r3)
    spread_modes(me, table, received, rows, mode_rows)
    coarse_rows[...] = coarse_rows_of(me, table, cases, received, coarse_rows.shape[1] // LANES)
    amplitude = first_amplitudes(gathered, coarse_rows[...], cases)
    lifted = lifted_by(amplitude, mode_rows)
    lifted_out[...] = lifted
    start = (table[PAD:PAD + cases, :] - lifted).astype(jnp.bfloat16)
    values_out[...] = dot(start, pinv[...], ((1,), (0,)))
    send_all(pieces, packed_rows(components(mode_rows[...], values_out[...]), cases))
    sending = pltpu.make_async_copy(pieces, gather_out, gather_sem)
    sending.start()
    pack_blocks(me, codes_of(table, cases), values_out, (s0, s1, s2, s3))
    sending.wait()


def rho_kernel(table, scaled, smoothed, lifted, rho_out, initial):
    initial[...] = table[MODES + 1:MODES + 2, :] * lifted[...]
    rho_out[...] = case_sums(folded(scaled[...].astype(f32) * smoothed[...]))


def first_lift_kernel(offsets, gathered, coarse_rows, mode_rows, lifted, coarse):
    spread_coarse(coarse_rows[...], offsets, coarse)
    lifted[...] = lifted_by(amplitudes(gathered, coarse, lifted.shape[0]), mode_rows)


def lift_kernel(gathered, coarse, mode_rows, lifted):
    lifted[...] = lifted_by(amplitudes(gathered, coarse, lifted.shape[0]), mode_rows)


def third_kernel(table, values, lifted, mode_rows, schur, r0, r1, r2, r3,
                 values_out, scaled_out, gather_out, s0, s1, s2, s3, field, pieces, gather_sem):
    me = lax.axis_index("mod")
    cases = values.shape[0]
    codes = codes_of(table, cases)
    jump(me, codes, values, (r0, r1, r2, r3), field)
    scaled = (field[...] - lifted[...]).astype(jnp.bfloat16)
    scaled_out[...] = scaled
    smoothed = dot(scaled, schur[...], ((1,), (0,)))
    values_out[...] = smoothed
    rows = components(mode_rows[...], smoothed)
    send_all(pieces, packed_rows(rows, cases))
    sending = pltpu.make_async_copy(pieces, gather_out, gather_sem)
    sending.start()
    pack_blocks(me, codes, values_out, (s0, s1, s2, s3))
    sending.wait()


def fourth_kernel(table, values, lifted, rho, pinv, r0, r1, r2, r3, corrected_out, gather_out, field):
    me = lax.axis_index("mod")
    cases = values.shape[0]
    jump(me, codes_of(table, cases), values, (r0, r1, r2, r3), field)
    corrected = field[...] - lifted[...]
    corrected_out[...] = table[MODES + 1:MODES + 2, :] * corrected
    direction = corrected.astype(jnp.bfloat16)
    response = dot(direction, pinv[...], ((1,), (0,)))
    kappa = case_sums(folded(direction.astype(f32) * response))
    blank = jnp.zeros((1, LANES - 2 * cases), f32)
    gather_out[...] = jnp.broadcast_to(jnp.concatenate([kappa, rho[...], blank], axis=1), gather_out.shape)


def last_kernel(gathered, direction, initial, out):
    cases = direction.shape[0]
    sums = jnp.sum(gathered[...], axis=0, keepdims=True)
    stride = sums[:, cases:2 * cases] / sums[:, :cases]
    at_row = lax.broadcasted_iota(jnp.int32, (cases, cases), 0)
    at_lane = lax.broadcasted_iota(jnp.int32, (cases, cases), 1)
    column = jnp.sum(jnp.where(at_row == at_lane, stride, 0.0), axis=1, keepdims=True)
    out[...] = initial[...] + column * direction[...]


def call(kernel, arguments, outs, scratch=(), flops=None, in_hbm=(), out_any=()):
    vmem = pl.BlockSpec(memory_space=pltpu.VMEM)
    hbm = pl.BlockSpec(memory_space=pltpu.HBM)
    anywhere = pl.BlockSpec(memory_space=pl.ANY)
    cost = None
    if flops:
        cost = pl.CostEstimate(flops=int(flops), bytes_accessed=0, transcendentals=0)
    arguments = [
        pltpu.with_memory_space_constraint(argument, pltpu.HBM) if i in in_hbm else argument
        for i, argument in enumerate(arguments)
    ]
    outs = [out if isinstance(out, jax.ShapeDtypeStruct) else jax.ShapeDtypeStruct(out, f32) for out in outs]
    return pl.pallas_call(
        kernel,
        out_shape=outs,
        in_specs=[hbm if i in in_hbm else vmem for i in range(len(arguments))],
        out_specs=[anywhere if i in out_any else vmem for i in range(len(outs))],
        scratch_shapes=list(scratch),
        compiler_params=pltpu.CompilerParams(vmem_limit_bytes=24 * 1024 * 1024),
        cost_estimate=cost,
    )(*arguments)


def on_device(loads, modes, pinv, schur, coarse_inverse, connectors):
    cases, dofs = loads.shape
    count = coarse_inverse.shape[1] // MODES
    tiles = count * PAD // LANES
    routes = swap_routes(count)
    offsets = (1, -1, ACROSS, -ACROSS)
    rows = GROUPS * PAD
    piece = (count, PAD, GROUPS * cases)
    blocks = (MAXC, cases, BLOCK)
    field = (cases, dofs)

    def swapped(packs):
        ordered = sorted(range(GROUPS), key=lambda swap: PLACE[swap])
        return [lax.ppermute(pack, "mod", routes[swap]) for pack, swap in zip(packs, ordered)]

    def exchanged(pieces):
        return lax.all_to_all(pieces, "mod", 0, 0)

    dma = pltpu.SemaphoreType.DMA
    pieces_scratch = [pltpu.VMEM(piece, f32), dma]
    table_rows = PAD + cases + pl.cdiv(count * PAD, dofs) * PAD
    flat_connectors = connectors.transpose(1, 0, 2)
    table, pieces, *packs = call(
        first_kernel, (flat_connectors, loads, modes, coarse_inverse),
        [(table_rows, dofs), piece] + [(MAXC + tiles, PAD, LANES)] * 4,
        [pltpu.VMEM(flat_connectors.shape, jnp.int32), pltpu.VMEM(loads.shape, loads.dtype), pltpu.VMEM(modes.shape, f32),
         pltpu.VMEM(coarse_inverse.shape, f32), pltpu.VMEM(piece, f32), dma((4,)), dma],
        flops=AHEAD, in_hbm=(0, 1, 2, 3), out_any=(1,),
    )
    gathered, received = exchanged(pieces), swapped(packs)
    coarse_rows, mode_rows, lifted, values, pieces, *packs = call(
        second_kernel, (table, gathered, pinv, *received),
        [(rows, count * PAD),
         jax.ShapeDtypeStruct((2 * rows, dofs), jnp.bfloat16), field, field, piece] + [blocks] * 4,
        [pltpu.VMEM((rows, dofs), f32)] + pieces_scratch, out_any=(4,),
    )
    gathered, received = exchanged(pieces), swapped(packs)
    residual_lift, coarse = call(
        functools.partial(first_lift_kernel, offsets), (gathered, coarse_rows, mode_rows),
        [field, jax.ShapeDtypeStruct((2 * GROUPS * rows, count * PAD), jnp.bfloat16)], flops=AHEAD,
    )
    values, scaled, pieces, *packs = call(
        third_kernel, (table, values, residual_lift, mode_rows, schur, *received),
        [field, jax.ShapeDtypeStruct(field, jnp.bfloat16), piece] + [blocks] * 4,
        [pltpu.VMEM(field, f32)] + pieces_scratch, out_any=(2,),
    )
    gathered, received = exchanged(pieces), swapped(packs)
    rho, initial = call(rho_kernel, (table, scaled, values, lifted), [(1, cases), field])
    smoothed_lift, = call(lift_kernel, (gathered, coarse, mode_rows), [field], flops=AHEAD)
    direction, pieces = call(
        fourth_kernel, (table, values, smoothed_lift, rho, pinv, *received),
        [field, (count, LANES)], [pltpu.VMEM(field, f32)],
    )
    gathered = exchanged(pieces.reshape(count, 1, LANES)).reshape(count, LANES)
    return call(last_kernel, (gathered, direction, initial), [field])[0]


def solution(mesh):
    in_specs = (
        P(None, "mod"),
        P(None, "mod"),
        P("mod", None),
        P("mod", None),
        P("mod", None),
        P("mod", None, None),
    )
    return jax.shard_map(
        on_device, mesh=mesh, in_specs=in_specs, out_specs=P(None, "mod"), check_vma=False
    )
```

```python
import functools

import jax
import jax.numpy as jnp
from jax import lax
from jax.experimental import pallas as pl
from jax.experimental.pallas import tpu as pltpu
from jax.sharding import PartitionSpec as P

MODES = 6
MAXC = 2
ACROSS = 8
BLOCK = 128
LANES = 128
GROUPS = 4
PAD = 8

highest = lax.Precision.HIGHEST
f32 = jnp.float32


def dot(a, b, contract, precision=None):
    return lax.dot_general(a, b, (contract, ((), ())), precision=precision, preferred_element_type=f32)


def exact(a, b, contract):
    return dot(a, b, contract, highest)


def swap_of(group, me):
    if group < 2:
        return (me + group) % 2
    return 2 + (me // ACROSS + group) % 2


def heading_of(swap, me):
    if swap < 2:
        return 1 + (me + swap) % 2
    return 3 + (me // ACROSS + swap) % 2


def swap_routes(count):
    routes = [[], [], [], []]
    for i in range(count):
        for group, offset in enumerate((1, -1, ACROSS, -ACROSS)):
            j = i + offset
            if 0 <= j < count and (group >= 2 or i // ACROSS == j // ACROSS):
                routes[swap_of(group, i)].append((i, j))
    return routes


PLACE = (3, 1, 2, 0)
AHEAD = 2e9


def by_swap(places):
    return [places[PLACE[swap]] for swap in range(GROUPS)]


def block_lanes(b):
    return slice(b * BLOCK, (b + 1) * BLOCK)


def inverse_place(tile, cases, dofs):
    per_row = dofs // LANES
    return PAD + cases + tile // per_row * PAD, block_lanes(tile % per_row)


def codes_of(table, cases):
    count = table.shape[1] // BLOCK
    return [jnp.broadcast_to(table[MODES:MODES + 1, block_lanes(b)], (cases, BLOCK)) for b in range(count)]


def code_at(heading, slot):
    return jnp.asarray(2 * heading + slot, jnp.int32).astype(f32)


def own_modes(table):
    row_id = lax.broadcasted_iota(jnp.int32, (PAD, table.shape[1]), 0)
    return jnp.where(row_id < MODES, table[:PAD, :], 0.0)


def chosen(values, codes, code):
    found = jnp.zeros_like(values[0])
    for value, mine in zip(values, codes):
        found = jnp.where(mine == code, value, found)
    return found


def pack_blocks(me, codes, values, outs):
    blocks = [values[:, block_lanes(b)] for b in range(len(codes))]
    for swap, out in enumerate(by_swap(outs)):
        for slot in range(MAXC):
            out[slot] = chosen(blocks, codes, code_at(heading_of(swap, me), slot))


def arrived(me, received, at):
    received = by_swap(received)
    pieces = []
    for g in range(GROUPS):
        first, second = received[2 * (g // 2)], received[2 * (g // 2) + 1]
        pieces.append(jnp.where(swap_of(g, me) % 2 == 0, first[at], second[at]))
    return pieces


def jump(me, codes, values, received, out):
    theirs = [arrived(me, received, slot) for slot in range(MAXC)]
    for b, code in enumerate(codes):
        partner = jnp.zeros_like(code)
        for g in range(GROUPS):
            for slot in range(MAXC):
                partner = jnp.where(code == 2 * (g + 1) + slot, theirs[slot][g], partner)
        out[:, block_lanes(b)] = jnp.where(code >= 2, values[:, block_lanes(b)] - partner, 0.0)


def send_all(out, piece):
    for device in range(out.shape[0]):
        out[device] = piece


def packed_rows(rows, cases):
    return jnp.concatenate([rows[g * PAD:(g + 1) * PAD] for g in range(GROUPS)], axis=1)


def halves(values):
    high = values.astype(jnp.bfloat16)
    return high, (values - high.astype(f32)).astype(jnp.bfloat16)


def amplitudes(gathered, coarse, cases):
    flat = gathered[...].reshape(gathered.shape[0] * PAD, GROUPS * cases)
    wide = GROUPS * cases
    product = dot(coarse[...], jnp.concatenate(halves(flat), axis=1), ((1,), (0,)))
    product = product[:, :wide] + product[:, wide:]
    rows = GROUPS * PAD
    half = GROUPS * rows
    product = product[:half] + product[half:]
    total = product[:rows, :cases]
    for g in range(1, GROUPS):
        total = total + product[g * rows:(g + 1) * rows, g * cases:(g + 1) * cases]
    return total


def first_amplitudes(gathered, rows, cases):
    flat = gathered[...].reshape(gathered.shape[0] * PAD, GROUPS * cases)[:, :cases]
    product = dot(jnp.concatenate(halves(rows), axis=0), jnp.concatenate(halves(flat), axis=1), ((1,), (0,)))
    product = product[:, :cases] + product[:, cases:]
    return product[:GROUPS * PAD] + product[GROUPS * PAD:]


def lifted_by(amplitude, mode_rows):
    high, low = halves(amplitude)
    cases = amplitude.shape[1]
    left = jnp.concatenate([jnp.concatenate([high, high], axis=0), jnp.concatenate([low, low], axis=0)], axis=1)
    product = dot(left, mode_rows[...], ((0,), (0,)))
    return product[:cases] + product[cases:]


def components(rows, values):
    cases = values.shape[0]
    product = dot(rows, jnp.concatenate(halves(values), axis=0), ((1,), (1,)))
    product = product[:, :cases] + product[:, cases:]
    return product[:GROUPS * PAD] + product[GROUPS * PAD:]


def folded(product):
    total = product[:, :LANES]
    for k in range(1, product.shape[1] // LANES):
        total = total + product[:, k * LANES:(k + 1) * LANES]
    return total


def case_sums(fold):
    cases = fold.shape[0]
    at_row = lax.broadcasted_iota(jnp.int32, (cases, cases), 0)
    at_lane = lax.broadcasted_iota(jnp.int32, (cases, cases), 1)
    column = jnp.sum(fold, axis=1, keepdims=True)
    return jnp.sum(jnp.where(at_row == at_lane, column, 0.0), axis=0, keepdims=True)


def first_kernel(connectors_hbm, loads_hbm, modes_hbm, inverse_hbm, table, gather_out, s0, s1, s2, s3,
                 connectors, loads, modes, inverse, pieces, sems, gather_sem):
    me = lax.axis_index("mod")
    cases, dofs = loads.shape
    moves = [
        pltpu.make_async_copy(source, target, sems.at[i])
        for i, (source, target) in enumerate(
            ((loads_hbm, loads), (modes_hbm, modes), (inverse_hbm, inverse), (connectors_hbm, connectors))
        )
    ]
    for move in moves:
        move.start()
    for move in moves[:2]:
        move.wait()
    loads_end = PAD + cases
    own = jnp.concatenate([modes[...], jnp.zeros((PAD - MODES, dofs), f32)], axis=0)
    rows = dot(jnp.concatenate(halves(own), axis=0), loads[...], ((1,), (1,)))
    rows = rows[:PAD] + rows[PAD:]
    send_all(pieces, jnp.concatenate([rows, jnp.zeros((PAD, (GROUPS - 1) * cases), f32)], axis=1))
    sending = pltpu.make_async_copy(pieces, gather_out, gather_sem)
    sending.start()
    for move in moves[2:]:
        move.wait()
    code_row = (2 * connectors[0] + connectors[1]).astype(f32)
    sign_row = connectors[2].astype(f32)
    codes = [jnp.broadcast_to(code_row[:, b:b + 1], (PAD, BLOCK)) for b in range(dofs // BLOCK)]
    blocks = [own[:, block_lanes(b)] for b in range(len(codes))]
    tile_row = lax.broadcasted_iota(jnp.int32, (PAD, BLOCK), 0)
    for b, code in enumerate(codes):
        sign = jnp.broadcast_to(sign_row[:, b:b + 1], (PAD, BLOCK))
        last = jnp.where(tile_row == MODES, code, sign)
        table[:PAD, block_lanes(b)] = jnp.where(tile_row < MODES, blocks[b], last)
    table[PAD:loads_end, :] = loads[...].astype(f32)
    per_tile = LANES // PAD * MODES
    at_row = lax.broadcasted_iota(jnp.int32, (per_tile, LANES), 0)
    at_lane = lax.broadcasted_iota(jnp.int32, (per_tile, LANES), 1)
    spread = ((at_lane % PAD < MODES) & (at_lane // PAD * MODES + at_lane % PAD == at_row)).astype(f32)
    raw = jnp.concatenate([inverse[...], jnp.zeros((PAD - MODES, inverse.shape[1]), f32)], axis=0)
    tiles = [
        exact(raw[:, k * per_tile:(k + 1) * per_tile], spread, ((1,), (0,))) for k in range(s0.shape[0] - MAXC)
    ]
    for k, tile in enumerate(tiles):
        top, lanes = inverse_place(k, cases, dofs)
        table[top:top + PAD, lanes] = tile
    for swap, out in enumerate(by_swap((s0, s1, s2, s3))):
        for slot in range(MAXC):
            out[slot] = chosen(blocks, codes, code_at(heading_of(swap, me), slot))
        for k, tile in enumerate(tiles):
            out[MAXC + k] = tile
    sending.wait()


def spread_modes(me, table, received, rows, mode_rows):
    own = own_modes(table)
    row_id = lax.broadcasted_iota(jnp.int32, (PAD, BLOCK), 0)
    theirs = [arrived(me, received, slot) for slot in range(MAXC)]
    shifted = [pltpu.roll(own, MODES - 2 * g, 0) for g in range(3)]
    for b, code in enumerate(codes_of(table, PAD)):
        lanes = block_lanes(b)
        for g in range(GROUPS):
            tile = jnp.zeros((PAD, BLOCK), f32)
            for slot in range(MAXC):
                tile = jnp.where(code == 2 * (g + 1) + slot, -theirs[slot][g], tile)
            mine = jnp.where(code >= 2, shifted[g][:, lanes], 0.0) if g < 3 else jnp.zeros((PAD, BLOCK), f32)
            rows[g * PAD:(g + 1) * PAD, lanes] = jnp.where(row_id < MODES, tile, mine)
    high, low = halves(rows[...])
    for k, part in enumerate((high, low)):
        mode_rows[k * GROUPS * PAD:(k + 1) * GROUPS * PAD, :] = part


def coarse_rows_of(me, table, cases, received, tiles):
    row_id = lax.broadcasted_iota(jnp.int32, (PAD, LANES), 0)
    rows = []
    for k in range(tiles):
        top, lanes = inverse_place(k, cases, table.shape[1])
        own = table[top:top + PAD, lanes]
        theirs = arrived(me, received, MAXC + k)
        parts = []
        for g in range(GROUPS):
            ours = pltpu.roll(own, MODES - 2 * g, 0) if g < 3 else jnp.zeros((PAD, LANES), f32)
            parts.append(jnp.where(row_id < MODES, theirs[g], ours))
        rows.append(jnp.concatenate(parts, axis=0))
    return jnp.concatenate(rows, axis=1)


def spread_coarse(rows, offsets, coarse):
    total, width = rows.shape
    lane = lax.broadcasted_iota(jnp.int32, (total, width), 1) % PAD
    for g in range(GROUPS):
        near = pltpu.roll(rows, (-PAD * offsets[g]) % width, 1)
        own_part = pltpu.roll(rows, MODES - 2 * g, 1) if g < 3 else jnp.zeros((total, width), f32)
        high, low = halves(jnp.where(lane < MODES, near, own_part))
        coarse[g * total:(g + 1) * total] = high
        coarse[(GROUPS + g) * total:(GROUPS + g + 1) * total] = low


def second_kernel(table, gathered, pinv, r0, r1, r2, r3,
                  coarse_rows, mode_rows, lifted_out, values_out, gather_out, s0, s1, s2, s3, rows, pieces, gather_sem):
    me = lax.axis_index("mod")
    cases = values_out.shape[0]
    received = (r0, r1, r2, r3)
    spread_modes(me, table, received, rows, mode_rows)
    coarse_rows[...] = coarse_rows_of(me, table, cases, received, coarse_rows.shape[1] // LANES)
    amplitude = first_amplitudes(gathered, coarse_rows[...], cases)
    lifted = lifted_by(amplitude, mode_rows)
    start = (table[PAD:PAD + cases, :] - lifted).astype(jnp.bfloat16)
    values_out[...] = dot(start, pinv[...], ((1,), (0,)))
    send_all(pieces, packed_rows(components(mode_rows[...], values_out[...]), cases))
    sending = pltpu.make_async_copy(pieces, gather_out, gather_sem)
    sending.start()
    lifted_out[...] = lifted
    pack_blocks(me, codes_of(table, cases), values_out, (s0, s1, s2, s3))
    sending.wait()


def rho_kernel(table, scaled, smoothed, lifted, rho_out, initial):
    initial[...] = table[MODES + 1:MODES + 2, :] * lifted[...]
    rho_out[...] = case_sums(folded(scaled[...].astype(f32) * smoothed[...]))


def first_lift_kernel(offsets, gathered, coarse_rows, mode_rows, lifted, coarse):
    spread_coarse(coarse_rows[...], offsets, coarse)
    lifted[...] = lifted_by(amplitudes(gathered, coarse, lifted.shape[0]), mode_rows)


def lift_kernel(gathered, coarse, mode_rows, lifted):
    lifted[...] = lifted_by(amplitudes(gathered, coarse, lifted.shape[0]), mode_rows)


def third_kernel(table, values, lifted, mode_rows, schur, r0, r1, r2, r3,
                 values_out, scaled_out, gather_out, s0, s1, s2, s3, field, pieces, gather_sem):
    me = lax.axis_index("mod")
    cases = values.shape[0]
    codes = codes_of(table, cases)
    jump(me, codes, values, (r0, r1, r2, r3), field)
    scaled = (field[...] - lifted[...]).astype(jnp.bfloat16)
    smoothed = dot(scaled, schur[...], ((1,), (0,)))
    values_out[...] = smoothed
    rows = components(mode_rows[...], smoothed)
    send_all(pieces, packed_rows(rows, cases))
    sending = pltpu.make_async_copy(pieces, gather_out, gather_sem)
    sending.start()
    scaled_out[...] = scaled
    pack_blocks(me, codes, values_out, (s0, s1, s2, s3))
    sending.wait()


def fourth_kernel(table, values, lifted, rho, pinv, r0, r1, r2, r3, corrected_out, gather_out, field):
    me = lax.axis_index("mod")
    cases = values.shape[0]
    jump(me, codes_of(table, cases), values, (r0, r1, r2, r3), field)
    corrected = field[...] - lifted[...]
    corrected_out[...] = table[MODES + 1:MODES + 2, :] * corrected
    direction = corrected.astype(jnp.bfloat16)
    response = dot(direction, pinv[...], ((1,), (0,)))
    kappa = case_sums(folded(direction.astype(f32) * response))
    blank = jnp.zeros((1, LANES - 2 * cases), f32)
    gather_out[...] = jnp.broadcast_to(jnp.concatenate([kappa, rho[...], blank], axis=1), gather_out.shape)


def last_kernel(gathered, direction, initial, out):
    cases = direction.shape[0]
    sums = jnp.sum(gathered[...], axis=0, keepdims=True)
    stride = sums[:, cases:2 * cases] / sums[:, :cases]
    at_row = lax.broadcasted_iota(jnp.int32, (cases, cases), 0)
    at_lane = lax.broadcasted_iota(jnp.int32, (cases, cases), 1)
    column = jnp.sum(jnp.where(at_row == at_lane, stride, 0.0), axis=1, keepdims=True)
    out[...] = initial[...] + column * direction[...]


def call(kernel, arguments, outs, scratch=(), flops=None, in_hbm=(), out_any=()):
    vmem = pl.BlockSpec(memory_space=pltpu.VMEM)
    hbm = pl.BlockSpec(memory_space=pltpu.HBM)
    anywhere = pl.BlockSpec(memory_space=pl.ANY)
    cost = None
    if flops:
        cost = pl.CostEstimate(flops=int(flops), bytes_accessed=0, transcendentals=0)
    arguments = [
        pltpu.with_memory_space_constraint(argument, pltpu.HBM) if i in in_hbm else argument
        for i, argument in enumerate(arguments)
    ]
    outs = [out if isinstance(out, jax.ShapeDtypeStruct) else jax.ShapeDtypeStruct(out, f32) for out in outs]
    return pl.pallas_call(
        kernel,
        out_shape=outs,
        in_specs=[hbm if i in in_hbm else vmem for i in range(len(arguments))],
        out_specs=[anywhere if i in out_any else vmem for i in range(len(outs))],
        scratch_shapes=list(scratch),
        compiler_params=pltpu.CompilerParams(vmem_limit_bytes=24 * 1024 * 1024),
        cost_estimate=cost,
    )(*arguments)


def on_device(loads, modes, pinv, schur, coarse_inverse, connectors):
    cases, dofs = loads.shape
    count = coarse_inverse.shape[1] // MODES
    tiles = count * PAD // LANES
    routes = swap_routes(count)
    offsets = (1, -1, ACROSS, -ACROSS)
    rows = GROUPS * PAD
    piece = (count, PAD, GROUPS * cases)
    blocks = (MAXC, cases, BLOCK)
    field = (cases, dofs)

    def swapped(packs):
        ordered = sorted(range(GROUPS), key=lambda swap: PLACE[swap])
        return [lax.ppermute(pack, "mod", routes[swap]) for pack, swap in zip(packs, ordered)]

    def exchanged(pieces):
        return lax.all_to_all(pieces, "mod", 0, 0)

    dma = pltpu.SemaphoreType.DMA
    pieces_scratch = [pltpu.VMEM(piece, f32), dma]
    table_rows = PAD + cases + pl.cdiv(count * PAD, dofs) * PAD
    flat_connectors = connectors.transpose(1, 0, 2)
    table, pieces, *packs = call(
        first_kernel, (flat_connectors, loads, modes, coarse_inverse),
        [(table_rows, dofs), piece] + [(MAXC + tiles, PAD, LANES)] * 4,
        [pltpu.VMEM(flat_connectors.shape, jnp.int32), pltpu.VMEM(loads.shape, loads.dtype), pltpu.VMEM(modes.shape, f32),
         pltpu.VMEM(coarse_inverse.shape, f32), pltpu.VMEM(piece, f32), dma((4,)), dma],
        flops=AHEAD, in_hbm=(0, 1, 2, 3), out_any=(1,),
    )
    gathered, received = exchanged(pieces), swapped(packs)
    coarse_rows, mode_rows, lifted, values, pieces, *packs = call(
        second_kernel, (table, gathered, pinv, *received),
        [(rows, count * PAD),
         jax.ShapeDtypeStruct((2 * rows, dofs), jnp.bfloat16), field, field, piece] + [blocks] * 4,
        [pltpu.VMEM((rows, dofs), f32)] + pieces_scratch, out_any=(4,),
    )
    gathered, received = exchanged(pieces), swapped(packs)
    residual_lift, coarse = call(
        functools.partial(first_lift_kernel, offsets), (gathered, coarse_rows, mode_rows),
        [field, jax.ShapeDtypeStruct((2 * GROUPS * rows, count * PAD), jnp.bfloat16)], flops=AHEAD,
    )
    values, scaled, pieces, *packs = call(
        third_kernel, (table, values, residual_lift, mode_rows, schur, *received),
        [field, jax.ShapeDtypeStruct(field, jnp.bfloat16), piece] + [blocks] * 4,
        [pltpu.VMEM(field, f32)] + pieces_scratch, out_any=(2,),
    )
    gathered, received = exchanged(pieces), swapped(packs)
    rho, initial = call(rho_kernel, (table, scaled, values, lifted), [(1, cases), field])
    smoothed_lift, = call(lift_kernel, (gathered, coarse, mode_rows), [field], flops=AHEAD)
    direction, pieces = call(
        fourth_kernel, (table, values, smoothed_lift, rho, pinv, *received),
        [field, (count, LANES)], [pltpu.VMEM(field, f32)],
    )
    gathered = exchanged(pieces.reshape(count, 1, LANES)).reshape(count, LANES)
    return call(last_kernel, (gathered, direction, initial), [field])[0]


def solution(mesh):
    in_specs = (
        P(None, "mod"),
        P(None, "mod"),
        P("mod", None),
        P("mod", None),
        P("mod", None),
        P("mod", None, None),
    )
    return jax.shard_map(
        on_device, mesh=mesh, in_specs=in_specs, out_specs=P(None, "mod"), check_vma=False
    )
```

```python
import functools

import jax
import jax.numpy as jnp
from jax import lax
from jax.experimental import pallas as pl
from jax.experimental.pallas import tpu as pltpu
from jax.sharding import PartitionSpec as P

MODES = 6
MAXC = 2
ACROSS = 8
BLOCK = 128
LANES = 128
GROUPS = 4
PAD = 8

highest = lax.Precision.HIGHEST
f32 = jnp.float32


def dot(a, b, contract, precision=None):
    return lax.dot_general(a, b, (contract, ((), ())), precision=precision, preferred_element_type=f32)


def exact(a, b, contract):
    return dot(a, b, contract, highest)


def swap_of(group, me):
    if group < 2:
        return (me + group) % 2
    return 2 + (me // ACROSS + group) % 2


def heading_of(swap, me):
    if swap < 2:
        return 1 + (me + swap) % 2
    return 3 + (me // ACROSS + swap) % 2


def swap_routes(count):
    routes = [[], [], [], []]
    for i in range(count):
        for group, offset in enumerate((1, -1, ACROSS, -ACROSS)):
            j = i + offset
            if 0 <= j < count and (group >= 2 or i // ACROSS == j // ACROSS):
                routes[swap_of(group, i)].append((i, j))
    return routes


PLACE = (3, 1, 2, 0)
AHEAD = 2e9


def by_swap(places):
    return [places[PLACE[swap]] for swap in range(GROUPS)]


def block_lanes(b):
    return slice(b * BLOCK, (b + 1) * BLOCK)


def inverse_place(tile, cases, dofs):
    per_row = dofs // LANES
    return PAD + cases + tile // per_row * PAD, block_lanes(tile % per_row)


def codes_of(table, cases):
    count = table.shape[1] // BLOCK
    return [jnp.broadcast_to(table[MODES:MODES + 1, block_lanes(b)], (cases, BLOCK)) for b in range(count)]


def code_at(heading, slot):
    return jnp.asarray(2 * heading + slot, jnp.int32).astype(f32)


def own_modes(table):
    row_id = lax.broadcasted_iota(jnp.int32, (PAD, table.shape[1]), 0)
    return jnp.where(row_id < MODES, table[:PAD, :], 0.0)


def chosen(values, codes, code):
    found = jnp.zeros_like(values[0])
    for value, mine in zip(values, codes):
        found = jnp.where(mine == code, value, found)
    return found


def pack_blocks(me, codes, values, outs):
    blocks = [values[:, block_lanes(b)] for b in range(len(codes))]
    for swap, out in enumerate(by_swap(outs)):
        for slot in range(MAXC):
            out[slot] = chosen(blocks, codes, code_at(heading_of(swap, me), slot))


def arrived(me, received, at):
    received = by_swap(received)
    pieces = []
    for g in range(GROUPS):
        first, second = received[2 * (g // 2)], received[2 * (g // 2) + 1]
        pieces.append(jnp.where(swap_of(g, me) % 2 == 0, first[at], second[at]))
    return pieces


def jump(me, codes, values, received, out):
    theirs = [arrived(me, received, slot) for slot in range(MAXC)]
    for b, code in enumerate(codes):
        partner = jnp.zeros_like(code)
        for g in range(GROUPS):
            for slot in range(MAXC):
                partner = jnp.where(code == 2 * (g + 1) + slot, theirs[slot][g], partner)
        out[:, block_lanes(b)] = jnp.where(code >= 2, values[:, block_lanes(b)] - partner, 0.0)


def send_all(out, piece):
    for device in range(out.shape[0]):
        out[device] = piece


def packed_rows(rows, cases):
    return jnp.concatenate([rows[g * PAD:(g + 1) * PAD] for g in range(GROUPS)], axis=1)


def halves(values):
    high = values.astype(jnp.bfloat16)
    return high, (values - high.astype(f32)).astype(jnp.bfloat16)


def amplitudes(gathered, coarse, cases):
    flat = gathered[...].reshape(gathered.shape[0] * PAD, GROUPS * cases)
    wide = GROUPS * cases
    product = dot(coarse[...], jnp.concatenate(halves(flat), axis=1), ((1,), (0,)))
    product = product[:, :wide] + product[:, wide:]
    rows = GROUPS * PAD
    half = GROUPS * rows
    product = product[:half] + product[half:]
    total = product[:rows, :cases]
    for g in range(1, GROUPS):
        total = total + product[g * rows:(g + 1) * rows, g * cases:(g + 1) * cases]
    return total


def first_amplitudes(gathered, rows, cases):
    flat = gathered[...].reshape(gathered.shape[0] * PAD, GROUPS * cases)[:, :cases]
    product = dot(jnp.concatenate(halves(rows), axis=0), jnp.concatenate(halves(flat), axis=1), ((1,), (0,)))
    product = product[:, :cases] + product[:, cases:]
    return product[:GROUPS * PAD] + product[GROUPS * PAD:]


def lifted_by(amplitude, mode_rows):
    high, low = halves(amplitude)
    cases = amplitude.shape[1]
    left = jnp.concatenate([jnp.concatenate([high, high], axis=0), jnp.concatenate([low, low], axis=0)], axis=1)
    product = dot(left, mode_rows[...], ((0,), (0,)))
    return product[:cases] + product[cases:]


def components(rows, values):
    cases = values.shape[0]
    product = dot(rows, jnp.concatenate(halves(values), axis=0), ((1,), (1,)))
    product = product[:, :cases] + product[:, cases:]
    return product[:GROUPS * PAD] + product[GROUPS * PAD:]


def folded(product):
    total = product[:, :LANES]
    for k in range(1, product.shape[1] // LANES):
        total = total + product[:, k * LANES:(k + 1) * LANES]
    return total


def case_sums(fold):
    cases = fold.shape[0]
    at_row = lax.broadcasted_iota(jnp.int32, (cases, cases), 0)
    at_lane = lax.broadcasted_iota(jnp.int32, (cases, cases), 1)
    column = jnp.sum(fold, axis=1, keepdims=True)
    return jnp.sum(jnp.where(at_row == at_lane, column, 0.0), axis=0, keepdims=True)


def first_kernel(connectors_hbm, loads_hbm, modes_hbm, inverse_hbm, table, gather_out, s0, s1, s2, s3,
                 connectors, loads, modes, inverse, pieces, sems, gather_sem):
    me = lax.axis_index("mod")
    cases, dofs = loads.shape
    moves = [
        pltpu.make_async_copy(source, target, sems.at[i])
        for i, (source, target) in enumerate(
            ((loads_hbm, loads), (modes_hbm, modes), (inverse_hbm, inverse), (connectors_hbm, connectors))
        )
    ]
    for move in moves:
        move.start()
    for move in moves[:2]:
        move.wait()
    loads_end = PAD + cases
    own = jnp.concatenate([modes[...], jnp.zeros((PAD - MODES, dofs), f32)], axis=0)
    rows = dot(jnp.concatenate(halves(own), axis=0), loads[...], ((1,), (1,)))
    rows = rows[:PAD] + rows[PAD:]
    send_all(pieces, jnp.concatenate([rows, jnp.zeros((PAD, (GROUPS - 1) * cases), f32)], axis=1))
    sending = pltpu.make_async_copy(pieces, gather_out, gather_sem)
    sending.start()
    for move in moves[2:]:
        move.wait()
    code_row = (2 * connectors[0] + connectors[1]).astype(f32)
    sign_row = connectors[2].astype(f32)
    codes = [jnp.broadcast_to(code_row[:, b:b + 1], (PAD, BLOCK)) for b in range(dofs // BLOCK)]
    blocks = [own[:, block_lanes(b)] for b in range(len(codes))]
    tile_row = lax.broadcasted_iota(jnp.int32, (PAD, BLOCK), 0)
    for b, code in enumerate(codes):
        sign = jnp.broadcast_to(sign_row[:, b:b + 1], (PAD, BLOCK))
        last = jnp.where(tile_row == MODES, code, sign)
        table[:PAD, block_lanes(b)] = jnp.where(tile_row < MODES, blocks[b], last)
    table[PAD:loads_end, :] = loads[...].astype(f32)
    per_tile = LANES // PAD * MODES
    at_row = lax.broadcasted_iota(jnp.int32, (per_tile, LANES), 0)
    at_lane = lax.broadcasted_iota(jnp.int32, (per_tile, LANES), 1)
    spread = ((at_lane % PAD < MODES) & (at_lane // PAD * MODES + at_lane % PAD == at_row)).astype(f32)
    raw = jnp.concatenate([inverse[...], jnp.zeros((PAD - MODES, inverse.shape[1]), f32)], axis=0)
    tiles = [
        exact(raw[:, k * per_tile:(k + 1) * per_tile], spread, ((1,), (0,))) for k in range(s0.shape[0] - MAXC)
    ]
    for k, tile in enumerate(tiles):
        top, lanes = inverse_place(k, cases, dofs)
        table[top:top + PAD, lanes] = tile
    for swap, out in enumerate(by_swap((s0, s1, s2, s3))):
        for slot in range(MAXC):
            out[slot] = chosen(blocks, codes, code_at(heading_of(swap, me), slot))
        for k, tile in enumerate(tiles):
            out[MAXC + k] = tile
    sending.wait()


def spread_modes(me, table, received, rows, mode_rows):
    own = own_modes(table)
    row_id = lax.broadcasted_iota(jnp.int32, (PAD, BLOCK), 0)
    theirs = [arrived(me, received, slot) for slot in range(MAXC)]
    shifted = [pltpu.roll(own, MODES - 2 * g, 0) for g in range(3)]
    for b, code in enumerate(codes_of(table, PAD)):
        lanes = block_lanes(b)
        for g in range(GROUPS):
            tile = jnp.zeros((PAD, BLOCK), f32)
            for slot in range(MAXC):
                tile = jnp.where(code == 2 * (g + 1) + slot, -theirs[slot][g], tile)
            mine = jnp.where(code >= 2, shifted[g][:, lanes], 0.0) if g < 3 else jnp.zeros((PAD, BLOCK), f32)
            rows[g * PAD:(g + 1) * PAD, lanes] = jnp.where(row_id < MODES, tile, mine)
    high, low = halves(rows[...])
    for k, part in enumerate((high, low)):
        mode_rows[k * GROUPS * PAD:(k + 1) * GROUPS * PAD, :] = part


def coarse_rows_of(me, table, cases, received, tiles):
    row_id = lax.broadcasted_iota(jnp.int32, (PAD, LANES), 0)
    rows = []
    for k in range(tiles):
        top, lanes = inverse_place(k, cases, table.shape[1])
        own = table[top:top + PAD, lanes]
        theirs = arrived(me, received, MAXC + k)
        parts = []
        for g in range(GROUPS):
            ours = pltpu.roll(own, MODES - 2 * g, 0) if g < 3 else jnp.zeros((PAD, LANES), f32)
            parts.append(jnp.where(row_id < MODES, theirs[g], ours))
        rows.append(jnp.concatenate(parts, axis=0))
    return jnp.concatenate(rows, axis=1)


def spread_coarse(rows, offsets, coarse):
    total, width = rows.shape
    lane = lax.broadcasted_iota(jnp.int32, (total, width), 1) % PAD
    for g in range(GROUPS):
        near = pltpu.roll(rows, (-PAD * offsets[g]) % width, 1)
        own_part = pltpu.roll(rows, MODES - 2 * g, 1) if g < 3 else jnp.zeros((total, width), f32)
        high, low = halves(jnp.where(lane < MODES, near, own_part))
        coarse[g * total:(g + 1) * total] = high
        coarse[(GROUPS + g) * total:(GROUPS + g + 1) * total] = low


def second_kernel(table, gathered, pinv, r0, r1, r2, r3,
                  coarse_rows, mode_rows, lifted_out, values_out, gather_out, s0, s1, s2, s3, rows, pieces, gather_sem):
    me = lax.axis_index("mod")
    cases = values_out.shape[0]
    received = (r0, r1, r2, r3)
    spread_modes(me, table, received, rows, mode_rows)
    coarse_rows[...] = coarse_rows_of(me, table, cases, received, coarse_rows.shape[1] // LANES)
    amplitude = first_amplitudes(gathered, coarse_rows[...], cases)
    lifted = lifted_by(amplitude, mode_rows)
    start = (table[PAD:PAD + cases, :] - lifted).astype(jnp.bfloat16)
    values_out[...] = dot(start, pinv[...], ((1,), (0,)))
    send_all(pieces, packed_rows(components(mode_rows[...], values_out[...]), cases))
    sending = pltpu.make_async_copy(pieces, gather_out, gather_sem)
    sending.start()
    lifted_out[...] = lifted
    pack_blocks(me, codes_of(table, cases), values_out, (s0, s1, s2, s3))
    sending.wait()


def first_lift_kernel(offsets, gathered, coarse_rows, mode_rows, lifted, coarse):
    spread_coarse(coarse_rows[...], offsets, coarse)
    lifted[...] = lifted_by(amplitudes(gathered, coarse, lifted.shape[0]), mode_rows)


def last_lift_kernel(gathered, coarse, mode_rows, table, scaled, smoothed, first_lifted, lifted, rho_out, initial):
    lifted[...] = lifted_by(amplitudes(gathered, coarse, lifted.shape[0]), mode_rows)
    rho_out[...] = case_sums(folded(scaled[...].astype(f32) * smoothed[...]))
    initial[...] = table[MODES + 1:MODES + 2, :] * first_lifted[...]


def third_kernel(table, values, lifted, mode_rows, schur, r0, r1, r2, r3,
                 values_out, scaled_out, gather_out, s0, s1, s2, s3, field, pieces, gather_sem):
    me = lax.axis_index("mod")
    cases = values.shape[0]
    codes = codes_of(table, cases)
    jump(me, codes, values, (r0, r1, r2, r3), field)
    scaled = (field[...] - lifted[...]).astype(jnp.bfloat16)
    smoothed = dot(scaled, schur[...], ((1,), (0,)))
    values_out[...] = smoothed
    rows = components(mode_rows[...], smoothed)
    send_all(pieces, packed_rows(rows, cases))
    sending = pltpu.make_async_copy(pieces, gather_out, gather_sem)
    sending.start()
    scaled_out[...] = scaled
    pack_blocks(me, codes, values_out, (s0, s1, s2, s3))
    sending.wait()


def fourth_kernel(table, values, lifted, rho, pinv, r0, r1, r2, r3, corrected_out, gather_out, field):
    me = lax.axis_index("mod")
    cases = values.shape[0]
    jump(me, codes_of(table, cases), values, (r0, r1, r2, r3), field)
    corrected = field[...] - lifted[...]
    corrected_out[...] = table[MODES + 1:MODES + 2, :] * corrected
    direction = corrected.astype(jnp.bfloat16)
    response = dot(direction, pinv[...], ((1,), (0,)))
    kappa = case_sums(folded(direction.astype(f32) * response))
    blank = jnp.zeros((1, LANES - 2 * cases), f32)
    gather_out[...] = jnp.broadcast_to(jnp.concatenate([kappa, rho[...], blank], axis=1), gather_out.shape)


def last_kernel(gathered, direction, initial, out):
    cases = direction.shape[0]
    sums = jnp.sum(gathered[...], axis=0, keepdims=True)
    stride = sums[:, cases:2 * cases] / sums[:, :cases]
    at_row = lax.broadcasted_iota(jnp.int32, (cases, cases), 0)
    at_lane = lax.broadcasted_iota(jnp.int32, (cases, cases), 1)
    column = jnp.sum(jnp.where(at_row == at_lane, stride, 0.0), axis=1, keepdims=True)
    out[...] = initial[...] + column * direction[...]


def call(kernel, arguments, outs, scratch=(), flops=None, in_hbm=(), out_any=()):
    vmem = pl.BlockSpec(memory_space=pltpu.VMEM)
    hbm = pl.BlockSpec(memory_space=pltpu.HBM)
    anywhere = pl.BlockSpec(memory_space=pl.ANY)
    cost = None
    if flops:
        cost = pl.CostEstimate(flops=int(flops), bytes_accessed=0, transcendentals=0)
    arguments = [
        pltpu.with_memory_space_constraint(argument, pltpu.HBM) if i in in_hbm else argument
        for i, argument in enumerate(arguments)
    ]
    outs = [out if isinstance(out, jax.ShapeDtypeStruct) else jax.ShapeDtypeStruct(out, f32) for out in outs]
    return pl.pallas_call(
        kernel,
        out_shape=outs,
        in_specs=[hbm if i in in_hbm else vmem for i in range(len(arguments))],
        out_specs=[anywhere if i in out_any else vmem for i in range(len(outs))],
        scratch_shapes=list(scratch),
        compiler_params=pltpu.CompilerParams(vmem_limit_bytes=24 * 1024 * 1024),
        cost_estimate=cost,
    )(*arguments)


def on_device(loads, modes, pinv, schur, coarse_inverse, connectors):
    cases, dofs = loads.shape
    count = coarse_inverse.shape[1] // MODES
    tiles = count * PAD // LANES
    routes = swap_routes(count)
    offsets = (1, -1, ACROSS, -ACROSS)
    rows = GROUPS * PAD
    piece = (count, PAD, GROUPS * cases)
    blocks = (MAXC, cases, BLOCK)
    field = (cases, dofs)

    def swapped(packs):
        ordered = sorted(range(GROUPS), key=lambda swap: PLACE[swap])
        return [lax.ppermute(pack, "mod", routes[swap]) for pack, swap in zip(packs, ordered)]

    def exchanged(pieces):
        return lax.all_to_all(pieces, "mod", 0, 0)

    dma = pltpu.SemaphoreType.DMA
    pieces_scratch = [pltpu.VMEM(piece, f32), dma]
    table_rows = PAD + cases + pl.cdiv(count * PAD, dofs) * PAD
    flat_connectors = connectors.transpose(1, 0, 2)
    table, pieces, *packs = call(
        first_kernel, (flat_connectors, loads, modes, coarse_inverse),
        [(table_rows, dofs), piece] + [(MAXC + tiles, PAD, LANES)] * 4,
        [pltpu.VMEM(flat_connectors.shape, jnp.int32), pltpu.VMEM(loads.shape, loads.dtype), pltpu.VMEM(modes.shape, f32),
         pltpu.VMEM(coarse_inverse.shape, f32), pltpu.VMEM(piece, f32), dma((4,)), dma],
        flops=AHEAD, in_hbm=(0, 1, 2, 3), out_any=(1,),
    )
    gathered, received = exchanged(pieces), swapped(packs)
    coarse_rows, mode_rows, lifted, values, pieces, *packs = call(
        second_kernel, (table, gathered, pinv, *received),
        [(rows, count * PAD),
         jax.ShapeDtypeStruct((2 * rows, dofs), jnp.bfloat16), field, field, piece] + [blocks] * 4,
        [pltpu.VMEM((rows, dofs), f32)] + pieces_scratch, out_any=(4,),
    )
    gathered, received = exchanged(pieces), swapped(packs)
    residual_lift, coarse = call(
        functools.partial(first_lift_kernel, offsets), (gathered, coarse_rows, mode_rows),
        [field, jax.ShapeDtypeStruct((2 * GROUPS * rows, count * PAD), jnp.bfloat16)], flops=AHEAD,
    )
    values, scaled, pieces, *packs = call(
        third_kernel, (table, values, residual_lift, mode_rows, schur, *received),
        [field, jax.ShapeDtypeStruct(field, jnp.bfloat16), piece] + [blocks] * 4,
        [pltpu.VMEM(field, f32)] + pieces_scratch, out_any=(2,),
    )
    gathered, received = exchanged(pieces), swapped(packs)
    smoothed_lift, rho, initial = call(
        last_lift_kernel, (gathered, coarse, mode_rows, table, scaled, values, lifted), [field, (1, cases), field], flops=AHEAD,
    )
    direction, pieces = call(
        fourth_kernel, (table, values, smoothed_lift, rho, pinv, *received),
        [field, (count, LANES)], [pltpu.VMEM(field, f32)],
    )
    gathered = exchanged(pieces.reshape(count, 1, LANES)).reshape(count, LANES)
    return call(last_kernel, (gathered, direction, initial), [field])[0]


def solution(mesh):
    in_specs = (
        P(None, "mod"),
        P(None, "mod"),
        P("mod", None),
        P("mod", None),
        P("mod", None),
        P("mod", None, None),
    )
    return jax.shard_map(
        on_device, mesh=mesh, in_specs=in_specs, out_specs=P(None, "mod"), check_vma=False
    )
```

```python
import functools

import jax
import jax.numpy as jnp
from jax import lax
from jax.experimental import pallas as pl
from jax.experimental.pallas import tpu as pltpu
from jax.sharding import PartitionSpec as P

MODES = 6
MAXC = 2
ACROSS = 8
BLOCK = 128
LANES = 128
GROUPS = 4
PAD = 8

highest = lax.Precision.HIGHEST
f32 = jnp.float32


def dot(a, b, contract, precision=None):
    return lax.dot_general(a, b, (contract, ((), ())), precision=precision, preferred_element_type=f32)


def exact(a, b, contract):
    return dot(a, b, contract, highest)


def swap_of(group, me):
    if group < 2:
        return (me + group) % 2
    return 2 + (me // ACROSS + group) % 2


def heading_of(swap, me):
    if swap < 2:
        return 1 + (me + swap) % 2
    return 3 + (me // ACROSS + swap) % 2


def swap_routes(count):
    routes = [[], [], [], []]
    for i in range(count):
        for group, offset in enumerate((1, -1, ACROSS, -ACROSS)):
            j = i + offset
            if 0 <= j < count and (group >= 2 or i // ACROSS == j // ACROSS):
                routes[swap_of(group, i)].append((i, j))
    return routes


PLACE = (3, 1, 2, 0)
AHEAD = 2e9


def by_swap(places):
    return [places[PLACE[swap]] for swap in range(GROUPS)]


def block_lanes(b):
    return slice(b * BLOCK, (b + 1) * BLOCK)


def inverse_place(tile, cases, dofs):
    per_row = dofs // LANES
    return PAD + cases + tile // per_row * PAD, block_lanes(tile % per_row)


def codes_of(table, cases):
    count = table.shape[1] // BLOCK
    return [jnp.broadcast_to(table[MODES:MODES + 1, block_lanes(b)], (cases, BLOCK)) for b in range(count)]


def code_at(heading, slot):
    return jnp.asarray(2 * heading + slot, jnp.int32).astype(f32)


def own_modes(table):
    row_id = lax.broadcasted_iota(jnp.int32, (PAD, table.shape[1]), 0)
    return jnp.where(row_id < MODES, table[:PAD, :], 0.0)


def chosen(values, codes, code):
    found = jnp.zeros_like(values[0])
    for value, mine in zip(values, codes):
        found = jnp.where(mine == code, value, found)
    return found


def pack_blocks(me, codes, values, outs):
    blocks = [values[:, block_lanes(b)] for b in range(len(codes))]
    for swap, out in enumerate(by_swap(outs)):
        for slot in range(MAXC):
            out[slot] = chosen(blocks, codes, code_at(heading_of(swap, me), slot))


def arrived(me, received, at):
    received = by_swap(received)
    pieces = []
    for g in range(GROUPS):
        first, second = received[2 * (g // 2)], received[2 * (g // 2) + 1]
        pieces.append(jnp.where(swap_of(g, me) % 2 == 0, first[at], second[at]))
    return pieces


def jump(me, codes, values, received, out):
    theirs = [arrived(me, received, slot) for slot in range(MAXC)]
    for b, code in enumerate(codes):
        partner = jnp.zeros_like(code)
        for g in range(GROUPS):
            for slot in range(MAXC):
                partner = jnp.where(code == 2 * (g + 1) + slot, theirs[slot][g], partner)
        out[:, block_lanes(b)] = jnp.where(code >= 2, values[:, block_lanes(b)] - partner, 0.0)


def send_all(out, piece):
    for device in range(out.shape[0]):
        out[device] = piece


def packed_rows(rows, cases):
    return jnp.concatenate([rows[g * PAD:(g + 1) * PAD] for g in range(GROUPS)], axis=1)


def halves(values):
    high = values.astype(jnp.bfloat16)
    return high, (values - high.astype(f32)).astype(jnp.bfloat16)


def amplitudes(gathered, coarse, cases):
    flat = gathered[...].reshape(gathered.shape[0] * PAD, GROUPS * cases)
    wide = GROUPS * cases
    product = dot(coarse[...], jnp.concatenate(halves(flat), axis=1), ((1,), (0,)))
    product = product[:, :wide] + product[:, wide:]
    rows = GROUPS * PAD
    half = GROUPS * rows
    product = product[:half] + product[half:]
    total = product[:rows, :cases]
    for g in range(1, GROUPS):
        total = total + product[g * rows:(g + 1) * rows, g * cases:(g + 1) * cases]
    return total


def first_amplitudes(gathered, rows, cases):
    flat = gathered[...].reshape(gathered.shape[0] * PAD, GROUPS * cases)[:, :cases]
    product = dot(jnp.concatenate(halves(rows), axis=0), jnp.concatenate(halves(flat), axis=1), ((1,), (0,)))
    product = product[:, :cases] + product[:, cases:]
    return product[:GROUPS * PAD] + product[GROUPS * PAD:]


def lifted_by(amplitude, mode_rows):
    high, low = halves(amplitude)
    cases = amplitude.shape[1]
    left = jnp.concatenate([jnp.concatenate([high, high], axis=0), jnp.concatenate([low, low], axis=0)], axis=1)
    product = dot(left, mode_rows[...], ((0,), (0,)))
    return product[:cases] + product[cases:]


def components(rows, values):
    cases = values.shape[0]
    product = dot(rows, jnp.concatenate(halves(values), axis=0), ((1,), (1,)))
    product = product[:, :cases] + product[:, cases:]
    return product[:GROUPS * PAD] + product[GROUPS * PAD:]


def folded(product):
    total = product[:, :LANES]
    for k in range(1, product.shape[1] // LANES):
        total = total + product[:, k * LANES:(k + 1) * LANES]
    return total


def case_sums(fold):
    cases = fold.shape[0]
    at_row = lax.broadcasted_iota(jnp.int32, (cases, cases), 0)
    at_lane = lax.broadcasted_iota(jnp.int32, (cases, cases), 1)
    column = jnp.sum(fold, axis=1, keepdims=True)
    return jnp.sum(jnp.where(at_row == at_lane, column, 0.0), axis=0, keepdims=True)


def first_kernel(connectors_hbm, loads_hbm, modes_hbm, inverse_hbm, table, gather_out, s0, s1, s2, s3,
                 connectors, loads, modes, inverse, pieces, sems, gather_sem):
    me = lax.axis_index("mod")
    cases, dofs = loads.shape
    moves = [
        pltpu.make_async_copy(source, target, sems.at[i])
        for i, (source, target) in enumerate(
            ((loads_hbm, loads), (modes_hbm, modes), (inverse_hbm, inverse), (connectors_hbm, connectors))
        )
    ]
    for move in moves:
        move.start()
    for move in moves[:2]:
        move.wait()
    loads_end = PAD + cases
    own = jnp.concatenate([modes[...], jnp.zeros((PAD - MODES, dofs), f32)], axis=0)
    rows = dot(jnp.concatenate(halves(own), axis=0), loads[...], ((1,), (1,)))
    rows = rows[:PAD] + rows[PAD:]
    send_all(pieces, jnp.concatenate([rows, jnp.zeros((PAD, (GROUPS - 1) * cases), f32)], axis=1))
    sending = pltpu.make_async_copy(pieces, gather_out, gather_sem)
    sending.start()
    for move in moves[2:]:
        move.wait()
    code_row = (2 * connectors[0] + connectors[1]).astype(f32)
    sign_row = connectors[2].astype(f32)
    codes = [jnp.broadcast_to(code_row[:, b:b + 1], (PAD, BLOCK)) for b in range(dofs // BLOCK)]
    blocks = [own[:, block_lanes(b)] for b in range(len(codes))]
    tile_row = lax.broadcasted_iota(jnp.int32, (PAD, BLOCK), 0)
    for b, code in enumerate(codes):
        sign = jnp.broadcast_to(sign_row[:, b:b + 1], (PAD, BLOCK))
        last = jnp.where(tile_row == MODES, code, sign)
        table[:PAD, block_lanes(b)] = jnp.where(tile_row < MODES, blocks[b], last)
    table[PAD:loads_end, :] = loads[...].astype(f32)
    per_tile = LANES // PAD * MODES
    at_row = lax.broadcasted_iota(jnp.int32, (per_tile, LANES), 0)
    at_lane = lax.broadcasted_iota(jnp.int32, (per_tile, LANES), 1)
    spread = ((at_lane % PAD < MODES) & (at_lane // PAD * MODES + at_lane % PAD == at_row)).astype(f32)
    raw = jnp.concatenate([inverse[...], jnp.zeros((PAD - MODES, inverse.shape[1]), f32)], axis=0)
    tiles = [
        exact(raw[:, k * per_tile:(k + 1) * per_tile], spread, ((1,), (0,))) for k in range(s0.shape[0] - MAXC)
    ]
    for k, tile in enumerate(tiles):
        top, lanes = inverse_place(k, cases, dofs)
        table[top:top + PAD, lanes] = tile
    for swap, out in enumerate(by_swap((s0, s1, s2, s3))):
        for slot in range(MAXC):
            out[slot] = chosen(blocks, codes, code_at(heading_of(swap, me), slot))
        for k, tile in enumerate(tiles):
            out[MAXC + k] = tile
    sending.wait()


def spread_modes(me, table, received, rows, mode_rows):
    own = own_modes(table)
    row_id = lax.broadcasted_iota(jnp.int32, (PAD, BLOCK), 0)
    theirs = [arrived(me, received, slot) for slot in range(MAXC)]
    shifted = [pltpu.roll(own, MODES - 2 * g, 0) for g in range(3)]
    for b, code in enumerate(codes_of(table, PAD)):
        lanes = block_lanes(b)
        for g in range(GROUPS):
            tile = jnp.zeros((PAD, BLOCK), f32)
            for slot in range(MAXC):
                tile = jnp.where(code == 2 * (g + 1) + slot, -theirs[slot][g], tile)
            mine = jnp.where(code >= 2, shifted[g][:, lanes], 0.0) if g < 3 else jnp.zeros((PAD, BLOCK), f32)
            rows[g * PAD:(g + 1) * PAD, lanes] = jnp.where(row_id < MODES, tile, mine)
    high, low = halves(rows[...])
    for k, part in enumerate((high, low)):
        mode_rows[k * GROUPS * PAD:(k + 1) * GROUPS * PAD, :] = part


def coarse_rows_of(me, table, cases, received, tiles):
    row_id = lax.broadcasted_iota(jnp.int32, (PAD, LANES), 0)
    rows = []
    for k in range(tiles):
        top, lanes = inverse_place(k, cases, table.shape[1])
        own = table[top:top + PAD, lanes]
        theirs = arrived(me, received, MAXC + k)
        parts = []
        for g in range(GROUPS):
            ours = pltpu.roll(own, MODES - 2 * g, 0) if g < 3 else jnp.zeros((PAD, LANES), f32)
            parts.append(jnp.where(row_id < MODES, theirs[g], ours))
        rows.append(jnp.concatenate(parts, axis=0))
    return jnp.concatenate(rows, axis=1)


def spread_coarse(rows, offsets, coarse):
    total, width = rows.shape
    lane = lax.broadcasted_iota(jnp.int32, (total, width), 1) % PAD
    for g in range(GROUPS):
        near = pltpu.roll(rows, (-PAD * offsets[g]) % width, 1)
        own_part = pltpu.roll(rows, MODES - 2 * g, 1) if g < 3 else jnp.zeros((total, width), f32)
        high, low = halves(jnp.where(lane < MODES, near, own_part))
        coarse[g * total:(g + 1) * total] = high
        coarse[(GROUPS + g) * total:(GROUPS + g + 1) * total] = low


def second_kernel(table, gathered, pinv, r0, r1, r2, r3,
                  coarse_rows, mode_rows, lifted_out, values_out, gather_out, s0, s1, s2, s3, rows, pieces, gather_sem):
    me = lax.axis_index("mod")
    cases = values_out.shape[0]
    received = (r0, r1, r2, r3)
    spread_modes(me, table, received, rows, mode_rows)
    plain = coarse_rows_of(me, table, cases, received, coarse_rows.shape[1] // LANES)
    coarse_rows[...] = plain
    amplitude = first_amplitudes(gathered, plain, cases)
    lifted = lifted_by(amplitude, mode_rows)
    start = (table[PAD:PAD + cases, :] - lifted).astype(jnp.bfloat16)
    applied = dot(start, pinv[...], ((1,), (0,)))
    values_out[...] = applied
    send_all(pieces, packed_rows(components(mode_rows[...], applied), cases))
    sending = pltpu.make_async_copy(pieces, gather_out, gather_sem)
    sending.start()
    lifted_out[...] = lifted
    pack_blocks(me, codes_of(table, cases), values_out, (s0, s1, s2, s3))
    sending.wait()


def first_lift_kernel(offsets, gathered, coarse_rows, mode_rows, lifted, coarse):
    spread_coarse(coarse_rows[...], offsets, coarse)
    lifted[...] = lifted_by(amplitudes(gathered, coarse, lifted.shape[0]), mode_rows)


def last_lift_kernel(gathered, coarse, mode_rows, table, scaled, smoothed, first_lifted, lifted, rho_out, initial):
    lifted[...] = lifted_by(amplitudes(gathered, coarse, lifted.shape[0]), mode_rows)
    rho_out[...] = case_sums(folded(scaled[...].astype(f32) * smoothed[...]))
    initial[...] = table[MODES + 1:MODES + 2, :] * first_lifted[...]


def third_kernel(table, values, lifted, mode_rows, schur, r0, r1, r2, r3,
                 values_out, scaled_out, gather_out, s0, s1, s2, s3, field, pieces, gather_sem):
    me = lax.axis_index("mod")
    cases = values.shape[0]
    codes = codes_of(table, cases)
    jump(me, codes, values, (r0, r1, r2, r3), field)
    scaled = (field[...] - lifted[...]).astype(jnp.bfloat16)
    smoothed = dot(scaled, schur[...], ((1,), (0,)))
    values_out[...] = smoothed
    rows = components(mode_rows[...], smoothed)
    send_all(pieces, packed_rows(rows, cases))
    sending = pltpu.make_async_copy(pieces, gather_out, gather_sem)
    sending.start()
    scaled_out[...] = scaled
    pack_blocks(me, codes, values_out, (s0, s1, s2, s3))
    sending.wait()


def fourth_kernel(table, values, lifted, rho, pinv, r0, r1, r2, r3, corrected_out, gather_out, field):
    me = lax.axis_index("mod")
    cases = values.shape[0]
    jump(me, codes_of(table, cases), values, (r0, r1, r2, r3), field)
    corrected = field[...] - lifted[...]
    corrected_out[...] = table[MODES + 1:MODES + 2, :] * corrected
    direction = corrected.astype(jnp.bfloat16)
    response = dot(direction, pinv[...], ((1,), (0,)))
    kappa = case_sums(folded(direction.astype(f32) * response))
    blank = jnp.zeros((1, LANES - 2 * cases), f32)
    gather_out[...] = jnp.broadcast_to(jnp.concatenate([kappa, rho[...], blank], axis=1), gather_out.shape)


def last_kernel(gathered, direction, initial, out):
    cases = direction.shape[0]
    sums = jnp.sum(gathered[...], axis=0, keepdims=True)
    stride = sums[:, cases:2 * cases] / sums[:, :cases]
    at_row = lax.broadcasted_iota(jnp.int32, (cases, cases), 0)
    at_lane = lax.broadcasted_iota(jnp.int32, (cases, cases), 1)
    column = jnp.sum(jnp.where(at_row == at_lane, stride, 0.0), axis=1, keepdims=True)
    out[...] = initial[...] + column * direction[...]


def call(kernel, arguments, outs, scratch=(), flops=None, in_hbm=(), out_any=()):
    vmem = pl.BlockSpec(memory_space=pltpu.VMEM)
    hbm = pl.BlockSpec(memory_space=pltpu.HBM)
    anywhere = pl.BlockSpec(memory_space=pl.ANY)
    cost = None
    if flops:
        cost = pl.CostEstimate(flops=int(flops), bytes_accessed=0, transcendentals=0)
    arguments = [
        pltpu.with_memory_space_constraint(argument, pltpu.HBM) if i in in_hbm else argument
        for i, argument in enumerate(arguments)
    ]
    outs = [out if isinstance(out, jax.ShapeDtypeStruct) else jax.ShapeDtypeStruct(out, f32) for out in outs]
    return pl.pallas_call(
        kernel,
        out_shape=outs,
        in_specs=[hbm if i in in_hbm else vmem for i in range(len(arguments))],
        out_specs=[anywhere if i in out_any else vmem for i in range(len(outs))],
        scratch_shapes=list(scratch),
        compiler_params=pltpu.CompilerParams(vmem_limit_bytes=24 * 1024 * 1024),
        cost_estimate=cost,
    )(*arguments)


def on_device(loads, modes, pinv, schur, coarse_inverse, connectors):
    cases, dofs = loads.shape
    count = coarse_inverse.shape[1] // MODES
    tiles = count * PAD // LANES
    routes = swap_routes(count)
    offsets = (1, -1, ACROSS, -ACROSS)
    rows = GROUPS * PAD
    piece = (count, PAD, GROUPS * cases)
    blocks = (MAXC, cases, BLOCK)
    field = (cases, dofs)

    def swapped(packs):
        ordered = sorted(range(GROUPS), key=lambda swap: PLACE[swap])
        return [lax.ppermute(pack, "mod", routes[swap]) for pack, swap in zip(packs, ordered)]

    def exchanged(pieces):
        return lax.all_to_all(pieces, "mod", 0, 0)

    dma = pltpu.SemaphoreType.DMA
    pieces_scratch = [pltpu.VMEM(piece, f32), dma]
    table_rows = PAD + cases + pl.cdiv(count * PAD, dofs) * PAD
    flat_connectors = connectors.transpose(1, 0, 2)
    table, pieces, *packs = call(
        first_kernel, (flat_connectors, loads, modes, coarse_inverse),
        [(table_rows, dofs), piece] + [(MAXC + tiles, PAD, LANES)] * 4,
        [pltpu.VMEM(flat_connectors.shape, jnp.int32), pltpu.VMEM(loads.shape, loads.dtype), pltpu.VMEM(modes.shape, f32),
         pltpu.VMEM(coarse_inverse.shape, f32), pltpu.VMEM(piece, f32), dma((4,)), dma],
        flops=AHEAD, in_hbm=(0, 1, 2, 3), out_any=(1,),
    )
    gathered, received = exchanged(pieces), swapped(packs)
    coarse_rows, mode_rows, lifted, values, pieces, *packs = call(
        second_kernel, (table, gathered, pinv, *received),
        [(rows, count * PAD),
         jax.ShapeDtypeStruct((2 * rows, dofs), jnp.bfloat16), field, field, piece] + [blocks] * 4,
        [pltpu.VMEM((rows, dofs), f32)] + pieces_scratch, out_any=(4,),
    )
    gathered, received = exchanged(pieces), swapped(packs)
    residual_lift, coarse = call(
        functools.partial(first_lift_kernel, offsets), (gathered, coarse_rows, mode_rows),
        [field, jax.ShapeDtypeStruct((2 * GROUPS * rows, count * PAD), jnp.bfloat16)], flops=AHEAD,
    )
    values, scaled, pieces, *packs = call(
        third_kernel, (table, values, residual_lift, mode_rows, schur, *received),
        [field, jax.ShapeDtypeStruct(field, jnp.bfloat16), piece] + [blocks] * 4,
        [pltpu.VMEM(field, f32)] + pieces_scratch, out_any=(2,),
    )
    gathered, received = exchanged(pieces), swapped(packs)
    smoothed_lift, rho, initial = call(
        last_lift_kernel, (gathered, coarse, mode_rows, table, scaled, values, lifted), [field, (1, cases), field], flops=AHEAD,
    )
    direction, pieces = call(
        fourth_kernel, (table, values, smoothed_lift, rho, pinv, *received),
        [field, (count, LANES)], [pltpu.VMEM(field, f32)],
    )
    gathered = exchanged(pieces.reshape(count, 1, LANES)).reshape(count, LANES)
    return call(last_kernel, (gathered, direction, initial), [field])[0]


def solution(mesh):
    in_specs = (
        P(None, "mod"),
        P(None, "mod"),
        P("mod", None),
        P("mod", None),
        P("mod", None),
        P("mod", None, None),
    )
    return jax.shard_map(
        on_device, mesh=mesh, in_specs=in_specs, out_specs=P(None, "mod"), check_vma=False
    )
```
